32 devices in a mesh: seq: 16 (over z, y, x), chan: 2 (over core).
Axes of the slice: x: 2, y: 2, z: 4, core: 2. Of those that a mesh axis runs over, the one named last changes fastest.
Arguments:
- layer_input: bfloat16 [8192, 1024], P('seq', 'chan'), may hold values from -24 to 24
- gain_first: float32 [1024], replicated, may hold values from 0.5 to 1.5
- in_weight: bfloat16 [1024, 3, 1024], P(None, None, 'chan'), may hold values from -0.1875 to 0.1875
- short_weight: float32 [3, 3, 1024], P(None, None, 'chan'), may hold values from -3.5 to 3.5
- filt_in: bfloat16 [25, 64], replicated, may hold values from -4 to 4
- filt_bias: float32 [64], replicated, may hold values from -3.140625 to 3.140625
- filt_mid: bfloat16 [64, 64], replicated, may hold values from -1 to 1
- filt_out: bfloat16 [64, 1024], P(None, 'chan'), may hold values from -0.0625 to 0.0625
- decay_rate: float32 [1024], P('chan'), may hold values from 0.05 to 273.06667
- conv_bias: float32 [1024], P('chan'), may hold values from -4 to 4
- out_weight: bfloat16 [1024, 1024], P('chan'), may hold values from -0.25 to 0.25
- gain_second: float32 [1024], replicated, may hold values from 0.5 to 1.5
- up_weight: bfloat16 [1024, 4096], P(None, 'chan'), may hold values from -0.1875 to 0.1875
- down_weight: bfloat16 [4096, 1024], P('chan'), may hold values from -0.125 to 0.125
Outputs:
- block_out: bfloat16 [8192, 1024], P('seq', 'chan')
The draws below stay inside these ranges and needn't reach their ends.
All inputs are finite; a program needn't handle non-finite values.
Results may differ from the reference program's by a relative error of at most 0.01.
The reference program's roundings to bfloat16 on the way count: a program that leaves them out, or rounds other values in their place, can miss the bound.
Values may be sent and summed in bfloat16 or wider, within the bound.
No kernel may reach another device: no remote copies, remote signals or barrier semaphores. Data moves between devices by JAX's collectives and lax.ppermute only.
A program may use at most 128 MiB of HBM per device.

```python
import jax
import jax.numpy as jnp
from jax import lax

D = 1024
FF = 4096
FILT = 64
BANDS = 12
FEAT = 25
KSHORT = 3
LEN = 8192


def draw_layer_input(key, part):
    key_values, key_rows, key_cols = jax.random.split(key, 3)
    ramp_cols = jnp.arange(D, dtype=jnp.float32) / D
    col_level = jax.random.uniform(key_cols, (D,), jnp.float32)
    row_level = jax.random.uniform(key_rows, (LEN,), jnp.float32)
    values = jnp.clip(jax.random.normal(key_values, (LEN, D), jnp.float32), -3.5, 3.5)
    col_scale = jnp.exp(2.302585 * (0.5 * ramp_cols + 0.5 * col_level - 0.5))
    row_scale = jnp.exp(2.302585 * (0.5 * row_level - 0.25))
    return (values * row_scale[:, None] * col_scale[None, :]).astype(jnp.bfloat16)


def rates_from(key, fast_share):
    key_pick, key_slow, key_fast = jax.random.split(key, 3)
    picked = jax.random.bernoulli(key_pick, fast_share, (D,))
    slow_level = jax.random.uniform(key_slow, (D,), jnp.float32)
    slow_rates = jnp.exp(jnp.log(0.05) + slow_level * (jnp.log(2.3) - jnp.log(0.05)))
    fast_level = jax.random.uniform(key_fast, (D,), jnp.float32)
    fast_rates = LEN / (30.0 + 20.0 * fast_level)
    return jnp.where(picked, fast_rates, slow_rates).astype(jnp.float32)


def draw_decay_rate(key, part):
    key = jax.random.fold_in(key, 7)
    return rates_from(key, 0.3)


def with_spikes(array, own_key, source, target, blocks, factor):
    owner, partner = [(jnp.arange(array.shape[axis_at]) // (array.shape[axis_at] // blocks)).reshape([-1 if axis == axis_at else 1 for axis in range(array.ndim)]) for axis_at in (source, target)]
    chosen = jax.random.permutation(own_key, blocks)[partner]
    strong = (owner == chosen) | (owner == (partner + blocks // 2) % blocks)
    return jnp.where(strong, factor * array, array)


def levels(rng, extent, cuts, least, high):
    level, own = 1.0, jax.random.fold_in(rng, 6)
    for dim, shards_of in cuts:
        heights = jnp.exp(jax.random.uniform(jax.random.fold_in(own, dim), (shards_of,), jnp.float32, least / len(cuts), high / len(cuts)))
        level = level * jnp.repeat(heights, extent[dim] // shards_of).reshape([-1 if axis == dim else 1 for axis in range(len(extent))])
    return level


def bell_draw(key, dims, deviation, bound, cuts=(), held_as=jnp.bfloat16):
    array = deviation * jax.random.normal(key, dims, jnp.float32)
    if cuts:
        array = array * levels(key, dims, cuts, -0.22, 0.18)
    return jnp.clip(array, -bound, bound).astype(held_as)


def gaussian_with(key, extent, scale, reach, shards, heavy, kind=jnp.bfloat16):
    result = scale * jax.random.normal(key, extent, jnp.float32)
    if shards:
        result = result * levels(key, extent, shards, -0.22, 0.18)
    return jnp.clip(with_spikes(result, jax.random.fold_in(key, 3), *heavy), -reach, reach).astype(kind)


def setup_inputs(seed: int = 0) -> dict:
    arg_keys = jax.random.split(jax.random.key(seed), 15)
    return {
        "layer_input": draw_layer_input(jax.random.fold_in(arg_keys[14], 71), 0),
        "gain_first": jnp.clip(1.0 + 0.1 * jax.random.normal(arg_keys[1], (D,), jnp.float32), 0.5, 1.5),
        "in_weight": bell_draw(arg_keys[2], (D, 3, D), D ** -0.5, 0.1875, ((2, 2),)),
        "short_weight": bell_draw(arg_keys[3], (KSHORT, 3, D), KSHORT ** -0.5, 3.5, ((2, 2),), jnp.float32),
        "filt_in": bell_draw(arg_keys[4], (FEAT, FILT), 1.0, 4.0),
        "filt_bias": jnp.clip(jax.random.uniform(arg_keys[5], (FILT,), jnp.float32, -3.140625, 3.140625), -3.140625, 3.140625),
        "filt_mid": bell_draw(arg_keys[6], (FILT, FILT), 0.25, 1.0),
        "filt_out": bell_draw(arg_keys[7], (FILT, D), LEN ** -0.5, 0.0625, ((1, 2),)),
        "decay_rate": draw_decay_rate(jax.random.fold_in(arg_keys[14], 71), 0),
        "conv_bias": bell_draw(arg_keys[9], (D,), 1.0, 4.0, ((0, 2),), jnp.float32),
        "out_weight": gaussian_with(arg_keys[10], (D, D), D ** -0.5, 0.25, ((0, 2),), (0, 1, 2, 2.0)),
        "gain_second": jnp.clip(1.0 + 0.1 * jax.random.normal(arg_keys[11], (D,), jnp.float32), 0.5, 1.5),
        "up_weight": bell_draw(arg_keys[12], (D, FF), D ** -0.5, 0.1875, ((1, 2),)),
        "down_weight": gaussian_with(arg_keys[13], (FF, D), FF ** -0.5, 0.125, ((0, 2),), (0, 1, 2, 2.0)),
    }


EPS = 1e-05
TWO_PI = 6.283185307179586

def layer_norm(rows_in, gain_row):
    values = rows_in.astype(jnp.float32)
    row_mean = lax.optimization_barrier(jnp.mean(values, axis=-1, keepdims=True))
    centered = values - row_mean
    spread = lax.optimization_barrier(jnp.mean(centered * centered, axis=-1, keepdims=True))
    return (centered * lax.rsqrt(spread + EPS) * gain_row).astype(jnp.bfloat16)

def filter_hidden(positions, full_length, filt_in, filt_bias, filt_mid):
    powers = 2 ** jnp.arange(BANDS, dtype=jnp.int32)
    angles = (positions[None, :] * powers[:, None] % full_length).astype(jnp.float32) * (TWO_PI / full_length)
    ramp_row = positions.astype(jnp.float32)[None, :] / full_length
    features = jnp.concatenate([ramp_row, jnp.cos(angles), jnp.sin(angles)], 0).astype(jnp.bfloat16)
    first_layer = lax.dot_general(filt_in, features, (((0,), (0,)), ((), ())), preferred_element_type=jnp.float32)
    first_layer = jnp.sin(first_layer + filt_bias[:, None]).astype(jnp.bfloat16)
    second_layer = lax.dot_general(filt_mid, first_layer, (((0,), (0,)), ((), ())), preferred_element_type=jnp.float32)
    return jnp.sin(second_layer).astype(jnp.bfloat16)

def reference(layer_input, gain_first, in_weight, short_weight, filt_in, filt_bias, filt_mid, filt_out, decay_rate, conv_bias, out_weight, gain_second, up_weight, down_weight):
    normed = layer_norm(layer_input, gain_first)
    projected = jnp.dot(normed, in_weight.reshape(D, 3 * D), preferred_element_type=jnp.float32).astype(jnp.bfloat16)
    padded = jnp.concatenate([jnp.zeros((KSHORT - 1, 3 * D), jnp.bfloat16), projected], 0)
    padded = padded.astype(jnp.float32).reshape(LEN + KSHORT - 1, 3, D)
    shorted = short_weight[0] * padded[KSHORT - 1:]
    for lag_index in range(1, KSHORT):
        shorted = shorted + short_weight[lag_index] * padded[KSHORT - 1 - lag_index:KSHORT - 1 - lag_index + LEN]
    gate_out = shorted[:, 0]
    gate_in = shorted[:, 1]
    value_part = shorted[:, 2]
    gated_value = value_part * gate_in
    positions = jnp.arange(LEN, dtype=jnp.int32)
    second_layer = filter_hidden(positions, LEN, filt_in, filt_bias, filt_mid)
    response = lax.dot_general(second_layer, filt_out, (((0,), (0,)), ((), ())), preferred_element_type=jnp.float32)
    response = response * jnp.exp(-decay_rate[None, :] * (positions.astype(jnp.float32)[:, None] / LEN))
    spectrum = jnp.fft.rfft(gated_value, n=2 * LEN, axis=0) * jnp.fft.rfft(response, n=2 * LEN, axis=0)
    convolved = jnp.fft.irfft(spectrum, n=2 * LEN, axis=0)[:LEN].astype(jnp.float32)
    mixed_rows = ((convolved + conv_bias * gated_value) * gate_out).astype(jnp.bfloat16)
    attended = jnp.dot(mixed_rows, out_weight, preferred_element_type=jnp.float32)
    residual = (layer_input.astype(jnp.float32) + attended).astype(jnp.bfloat16)
    normed_second = layer_norm(residual, gain_second)
    hidden = jax.nn.gelu(jnp.dot(normed_second, up_weight, preferred_element_type=jnp.float32), approximate=False).astype(jnp.bfloat16)
    down_sums = jnp.dot(hidden, down_weight, preferred_element_type=jnp.float32)
    return (residual.astype(jnp.float32) + down_sums).astype(jnp.bfloat16)
```

```python
import functools

import jax
import jax.numpy as jnp
import ml_dtypes
import numpy as np
from jax import lax
from jax.experimental import pallas as pl
from jax.experimental.pallas import tpu as pltpu
from jax.sharding import PartitionSpec as P

BANDS = 12
KSHORT = 3
LANES = 128
HALO = 16
EPS = 1e-05
PI_HIGH = 3.140625
PI_LOW = 9.67653589793e-4
F32 = jnp.float32
BF16 = jnp.bfloat16
VMEM_BYTES = 60 * 1024 * 1024


def matmul(left, right):
    return jnp.dot(left, right, preferred_element_type=F32)


def split_parts(values):
    high = values.astype(BF16)
    return high, (values - high.astype(F32)).astype(BF16)


def split_table(table):
    high = table.astype(np.float32).astype(ml_dtypes.bfloat16)
    low = (table - high.astype(np.float64)).astype(np.float32).astype(ml_dtypes.bfloat16)
    return high, low


def transform_tables(length):
    rows = length // LANES
    period = 2 * rows
    full = 2 * length
    kept = rows + 1
    padded = -(-kept // 8) * 8
    k2 = np.arange(padded)
    valid = (k2 < kept).astype(np.float64)[:, None]
    n2 = np.arange(rows)
    n1 = np.arange(LANES)
    first = 2 * np.pi / period * (k2[:, None] * n2[None, :] % period)
    forward = np.concatenate([np.cos(first) * valid, -np.sin(first) * valid], 0)
    weight = np.where((k2 == 0) | (k2 == rows), 1.0, 2.0)[:, None] * valid
    inverse = np.concatenate([np.cos(first) * weight, -np.sin(first) * weight], 0).T
    turn = 2 * np.pi / full * (k2[:, None] * n1[None, :] % full)
    second = 2 * np.pi / LANES * (n1[:, None] * n1[None, :] % LANES)
    cos2, sin2 = np.cos(second), np.sin(second)
    mid = np.concatenate(
        [np.concatenate([cos2, -sin2], 1), np.concatenate([sin2, cos2], 1)], 0
    )
    back = np.concatenate(
        [np.concatenate([cos2, sin2], 1), np.concatenate([-sin2, cos2], 1)], 0
    ) / full
    f_high, f_low = split_table(forward)
    i_high, i_low = split_table(inverse)
    return {
        "forward2": np.concatenate([f_high, f_low], 1),
        "forward3": np.concatenate([f_high, f_high, f_low], 1),
        "inverse3": np.concatenate([i_high, i_high, i_low], 1),
        "turn_cos": np.tile(np.cos(turn), (1, 2)).astype(np.float32),
        "turn_sin": np.tile(np.sin(turn), (1, 2)).astype(np.float32),
        "mid": np.stack(split_table(mid)),
        "back": np.stack(split_table(back)),
    }


def sine(values):
    count = jnp.floor(values * (1.0 / np.pi) + 0.5)
    rest = (values - count * PI_HIGH) - count * PI_LOW
    half = count * 0.5
    sign = 1.0 - 4.0 * (half - jnp.floor(half))
    return sign * sine_poly(rest)


def sine_poly(rest):
    square = rest * rest
    poly = -2.5052108385441720e-08
    poly = poly * square + 2.7557319223985893e-06
    poly = poly * square - 1.9841269841269841e-04
    poly = poly * square + 8.3333333333333333e-03
    poly = poly * square - 1.6666666666666667e-01
    return rest + rest * square * poly


def sine_turns(turns):
    count = jnp.floor(turns * 2.0 + 0.5)
    rest = (turns - count * 0.5) * (2.0 * np.pi)
    half = count * 0.5
    sign = 1.0 - 4.0 * (half - jnp.floor(half))
    return sign * sine_poly(rest)


def rows_to_spectrum(load_pair, group, table_ref, turn_cos, turn_sin, mid_ref, padded):
    stacked = []
    for pair in range(group // 2):
        first = matmul(table_ref[...], load_pair(pair))
        real, imag = first[:padded], first[padded:]
        turned_real = real * turn_cos + imag * turn_sin
        turned_imag = imag * turn_cos - real * turn_sin
        for side in range(2):
            lanes = slice(side * LANES, (side + 1) * LANES)
            stacked.append(jnp.concatenate([turned_real[:, lanes], turned_imag[:, lanes]], 1))
    high, low = split_parts(jnp.concatenate(stacked, 0))
    return matmul(high, mid_ref[0]) + matmul(low, mid_ref[0]) + matmul(high, mid_ref[1])


def project_kernel(me_ref, *refs, pieces, tokens, width):
    x_refs, refs = refs[:pieces], refs[pieces:]
    halo_refs, refs = refs[:pieces], refs[pieces:]
    gain_ref, w_in_ref, w_value_ref, taps_ref, normed_ref, gated_ref, proj_ref = refs
    me = me_ref[0]
    places = [lax.rem(me + p, pieces) for p in range(pieces)]
    total = pieces * width

    def norm_rows(parts, start, size):
        values = [part.astype(F32) for part in parts]
        mean = sum(jnp.sum(v, axis=1, keepdims=True) for v in values) / total
        centered = [v - mean for v in values]
        spread = sum(jnp.sum(c * c, axis=1, keepdims=True) for c in centered) / total
        scale = lax.rsqrt(spread + EPS)
        for p in range(pieces):
            gain = gain_ref[places[p]]
            normed_ref[p, start : start + size, :] = (centered[p] * scale * gain).astype(BF16)

    norm_rows([ref[...] for ref in halo_refs], 0, HALO)
    chunk = 128
    for start in range(0, tokens, chunk):
        norm_rows([ref[start : start + chunk, :] for ref in x_refs], HALO + start, chunk)
    step = min(width, 256)
    for col in range(0, width, step):
        cols = slice(col, col + step)
        for role, w_ref in enumerate((w_in_ref, w_value_ref)):
            sums = 0.0
            for p in range(pieces):
                rows = pl.ds(pl.multiple_of(places[p] * width, width), width)
                sums = sums + matmul(normed_ref[p], w_ref[0, rows, cols])
            proj_ref[role] = sums.astype(BF16).astype(F32)
        shorted = []
        for role in range(2):
            value = taps_ref[0, role + 1 : role + 2, cols] * proj_ref[role, HALO : HALO + tokens, :]
            for lag in range(1, KSHORT):
                value = (
                    value
                    + taps_ref[lag, role + 1 : role + 2, cols]
                    * proj_ref[role, HALO - lag : HALO - lag + tokens, :]
                )
            shorted.append(value)
        gated = shorted[1] * shorted[0]
        gated_ref[cols, :] = gated.T.astype(BF16)


def gate_kernel(me_ref, normed_ref, *refs, pieces, share, width):
    w_refs, refs = refs[:pieces], refs[pieces:]
    tap_refs, refs = refs[:pieces], refs[pieces:]
    gate_ref, proj_ref = refs
    me = me_ref[0]
    places = [lax.rem(me + p, pieces) for p in range(pieces)]
    own = pl.ds(pl.multiple_of(me * share, 16), share + HALO)
    for out in range(pieces):
        sums = 0.0
        for p in range(pieces):
            rows = pl.ds(pl.multiple_of(places[p] * width, width), width)
            sums = sums + matmul(normed_ref[p, own, :], w_refs[out][0, rows, :])
        proj_ref[...] = sums.astype(BF16).astype(F32)
        value = tap_refs[out][0, 0:1, :] * proj_ref[HALO : HALO + share, :]
        for lag in range(1, KSHORT):
            value = value + tap_refs[out][lag, 0:1, :] * proj_ref[HALO - lag : HALO - lag + share, :]
        gate_ref[out] = value.T


def filter_kernel(
    in_ref, bias_ref, mid_w_ref, out_w_ref, decay_ref, forward_ref, cos_ref, sin_ref, mid_ref,
    spectrum_ref, response_ref, *, length, own, group, padded
):
    rows = length // LANES
    chunk = min(1024, length)
    feats = in_ref.shape[1]
    row_ids = lax.broadcasted_iota(jnp.int32, (feats, chunk), 0)
    band = jnp.where(row_ids > BANDS, row_ids - (BANDS + 1), row_ids - 1)
    band = jnp.clip(band, 0, BANDS - 1)
    quarter = jnp.where(row_ids <= BANDS, 0.25, 0.0)
    for start in range(0, length, chunk):
        places = lax.broadcasted_iota(jnp.int32, (feats, chunk), 1) + start
        phase = lax.shift_left(places, band) & (length - 1)
        turns = phase.astype(F32) * (1.0 / length)
        waves = sine_turns(turns + quarter)
        features = jnp.where(
            row_ids == 0,
            places.astype(F32) / length,
            jnp.where(row_ids <= 2 * BANDS, waves, 0.0),
        ).astype(BF16)
        first = sine(matmul(in_ref[...], features) + bias_ref[...]).astype(BF16)
        second = sine(matmul(mid_w_ref[...], first)).astype(BF16)
        ramp = (lax.broadcasted_iota(jnp.int32, (1, chunk), 1) + start).astype(F32) / length
        response = matmul(out_w_ref[...], second) * jnp.exp(-decay_ref[...] * ramp)
        for part in range(chunk // LANES):
            row = start // LANES + part
            response_ref[pl.ds(row, own, stride=rows), :] = response[:, part * LANES : (part + 1) * LANES]

    def one_group(step, carry):
        def load_pair(pair):
            base = (step * group + 2 * pair) * rows
            both = [
                response_ref[pl.ds(pl.multiple_of(base + side * rows, 8), rows), :] for side in range(2)
            ]
            high, low = split_parts(jnp.concatenate(both, 1))
            return jnp.concatenate([high, low, high], 0)

        spectrum = rows_to_spectrum(
            load_pair, group, forward_ref, cos_ref[...], sin_ref[...], mid_ref, padded
        )
        spectrum_ref[pl.ds(pl.multiple_of(step * group * padded, 8), group * padded), :] = spectrum
        return carry

    lax.fori_loop(0, own // group, one_group, 0)


def convolve_kernel(
    x_ref, spectrum_ref, bias_ref, forward_ref, inverse_ref, cos_ref, sin_ref, mid_ref, back_ref,
    out_ref, signal_ref, result_ref, *, length, own, group, padded, tokens, places
):
    rows = length // LANES
    per_block = tokens // LANES
    for row in range(rows):
        block, part = divmod(row, per_block)
        values = x_ref[block, :, part * LANES : (part + 1) * LANES].astype(F32)
        signal_ref[pl.ds(row, own, stride=rows), :] = values
    turn_cos, turn_sin = cos_ref[...], sin_ref[...]

    def one_group(step, carry):
        def load_pair(pair):
            base = (step * group + 2 * pair) * rows
            both = [
                signal_ref[pl.ds(pl.multiple_of(base + side * rows, 8), rows), :] for side in range(2)
            ]
            values = jnp.concatenate(both, 1).astype(BF16)
            return jnp.concatenate([values, values], 0)

        signal = rows_to_spectrum(load_pair, group, forward_ref, turn_cos, turn_sin, mid_ref, padded)
        other = spectrum_ref[pl.ds(pl.multiple_of(step * group * padded, 8), group * padded), :]
        s_real, s_imag = signal[:, :LANES], signal[:, LANES:]
        f_real, f_imag = other[:, :LANES], other[:, LANES:]
        product = jnp.concatenate(
            [s_real * f_real - s_imag * f_imag, s_real * f_imag + s_imag * f_real], 1
        )
        high, low = split_parts(product)
        mixed = matmul(high, back_ref[0]) + matmul(low, back_ref[0]) + matmul(high, back_ref[1])
        for pair in range(group // 2):
            first = mixed[2 * pair * padded : (2 * pair + 1) * padded]
            second = mixed[(2 * pair + 1) * padded : (2 * pair + 2) * padded]
            real = jnp.concatenate([first[:, :LANES], second[:, :LANES]], 1)
            imag = jnp.concatenate([first[:, LANES:], second[:, LANES:]], 1)
            turned = jnp.concatenate(
                [real * turn_cos - imag * turn_sin, imag * turn_cos + real * turn_sin], 0
            )
            t_high, t_low = split_parts(turned)
            values = matmul(inverse_ref[...], jnp.concatenate([t_high, t_low, t_high], 0))
            base = (step * group + 2 * pair) * rows
            for side in range(2):
                result_ref[pl.ds(pl.multiple_of(base + side * rows, 8), rows), :] = values[
                    :, side * LANES : (side + 1) * LANES
                ]
        return carry

    lax.fori_loop(0, own // group, one_group, 0)
    bias = bias_ref[...]
    share_rows = per_block // places
    for row in range(rows):
        block, part = divmod(row, per_block)
        place, lane = divmod(part, share_rows)
        values = result_ref[pl.ds(row, own, stride=rows), :]
        values = values + bias * x_ref[block, :, part * LANES : (part + 1) * LANES].astype(F32)
        target = place * (rows // per_block) + block
        out_ref[target, :, lane * LANES : (lane + 1) * LANES] = values.astype(BF16)


def gelu(values):
    return values * (lax.erf(values * np.float32(0.5**0.5)) + 1.0) * 0.5


def tail_kernel(me_ref, z_ref, gate_ref, gain_ref, *refs, pieces, share, width, steps):
    x_refs, refs = refs[:pieces], refs[pieces:]
    mix_refs, refs = refs[:pieces], refs[pieces:]
    up_refs, refs = refs[:pieces], refs[pieces:]
    down_refs, refs = refs[:pieces], refs[pieces:]
    out_ref, sums_ref, normed_ref = refs
    me = me_ref[0]
    places = [lax.rem(me + p, pieces) for p in range(pieces)]
    total = pieces * width
    dims = (((0,), (0,)), ((), ()))

    @pl.when(pl.program_id(0) == 0)
    def _():
        sums = 0.0
        for p in range(pieces):
            mixed = (z_ref[places[p]].astype(F32) * gate_ref[p]).astype(BF16)
            sums = sums + lax.dot_general(mixed, mix_refs[p][...], dims, preferred_element_type=F32)
        sums_ref[...] = sums
        own = pl.ds(pl.multiple_of(me * share, 16), share)
        for p in range(pieces):
            cols = pl.ds(pl.multiple_of(places[p] * width, LANES), width)
            residual = x_refs[p][own, :].astype(F32) + sums_ref[:, cols]
            sums_ref[:, cols] = residual.astype(BF16).astype(F32)
        values = sums_ref[...]
        mean = jnp.sum(values, axis=1, keepdims=True) / total
        centered = values - mean
        spread = jnp.sum(centered * centered, axis=1, keepdims=True) / total
        normed_ref[...] = (centered * lax.rsqrt(spread + EPS) * gain_ref[...]).astype(BF16)

    sums = sums_ref[...]
    for p in range(pieces):
        hidden = gelu(matmul(normed_ref[...], up_refs[p][...])).astype(BF16)
        sums = sums + matmul(hidden, down_refs[p][...])
    sums_ref[...] = sums

    @pl.when(pl.program_id(0) == steps - 1)
    def _():
        for p in range(pieces):
            cols = pl.ds(pl.multiple_of(places[p] * width, LANES), width)
            out_ref[p] = sums_ref[:, cols].astype(BF16)


def call(kernel, out_shape, scratch=(), **extra):
    return pl.pallas_call(
        kernel,
        out_shape=out_shape,
        scratch_shapes=list(scratch),
        compiler_params=pltpu.CompilerParams(vmem_limit_bytes=VMEM_BYTES),
        **extra,
    )


def shape_of(shape, dtype):
    return jax.ShapeDtypeStruct(shape, dtype)


SCALAR = pl.BlockSpec(memory_space=pltpu.SMEM)
WHOLE = pl.BlockSpec(memory_space=pltpu.VMEM)


def per_device(
    layer_input, gain_first, in_weight, short_weight, filt_in, filt_bias, filt_mid, filt_out,
    decay_rate, conv_bias, out_weight, gain_second, up_weight, down_weight,
):
    tokens, width = layer_input.shape
    pieces = lax.axis_size("chan")
    groups = lax.axis_size("seq")
    seq_place = lax.axis_index("seq")
    chan_place = lax.axis_index("chan")
    model = pieces * width
    length = tokens * groups
    share = tokens // pieces
    own = width // groups
    me = chan_place.astype(jnp.int32).reshape(1)

    def turned(array, by):
        if by == 0:
            return array
        return lax.ppermute(array, "chan", [(i, (i - by) % pieces) for i in range(pieces)])

    def all_turned(array):
        return [turned(array, p) for p in range(pieces)]

    x_pieces = all_turned(layer_input)
    last_rows = layer_input[tokens - HALO :]
    halo_pieces = [
        lax.ppermute(
            last_rows,
            ("seq", "chan"),
            [
                (s * pieces + i, (s + 1) * pieces + (i - p) % pieces)
                for s in range(groups - 1)
                for i in range(pieces)
            ],
        )
        for p in range(pieces)
    ]
    by_role = jnp.transpose(in_weight, (1, 0, 2))
    gain_pieces = gain_first.reshape(pieces, 1, width)

    def role_spec(role):
        return pl.BlockSpec((1, model, width), lambda i, role=role: (role, 0, 0))

    def full_spec(shape):
        return pl.BlockSpec(shape, lambda i: (0,) * len(shape))

    normed, gated = call(
        functools.partial(project_kernel, pieces=pieces, tokens=tokens, width=width),
        (shape_of((pieces, tokens + HALO, width), BF16), shape_of((width, tokens), BF16)),
        [pltpu.VMEM((2, tokens + HALO, min(width, 256)), F32)],
        grid=(1,),
        in_specs=[SCALAR]
        + [full_spec((tokens, width))] * pieces
        + [full_spec((HALO, width))] * pieces
        + [full_spec((pieces, 1, width)), role_spec(1), role_spec(2), full_spec(short_weight.shape)],
        out_specs=(full_spec((pieces, tokens + HALO, width)), full_spec((width, tokens))),
    )(me, *x_pieces, *halo_pieces, gain_pieces, by_role, by_role, short_weight)

    regrouped = lax.all_to_all(
        gated.reshape(groups, own, tokens), "seq", split_axis=0, concat_axis=0, tiled=True
    )

    tables = transform_tables(length)
    padded = tables["turn_cos"].shape[0]
    rows = length // LANES
    group = min(8, own)
    feats = 2 * BANDS + 1
    in_columns = jnp.pad(filt_in, ((0, 32 - feats), (0, 0))).T
    own_out = lax.dynamic_slice_in_dim(filt_out, seq_place * own, own, 1).T
    own_decay = lax.dynamic_slice_in_dim(decay_rate, seq_place * own, own, 0)[:, None]
    own_bias = lax.dynamic_slice_in_dim(conv_bias, seq_place * own, own, 0)[:, None]
    spectrum = call(
        functools.partial(filter_kernel, length=length, own=own, group=group, padded=padded),
        shape_of((own * padded, 2 * LANES), F32),
        [pltpu.VMEM((own * rows, LANES), F32)],
    )(
        in_columns, filt_bias[:, None], filt_mid.T, own_out, own_decay,
        tables["forward3"], tables["turn_cos"], tables["turn_sin"], tables["mid"],
    )

    gate_weights = all_turned(by_role[:1])
    gate_taps = all_turned(short_weight[:, :1])
    mix_weights = all_turned(out_weight)
    up_weights = all_turned(up_weight)
    down_weights = all_turned(down_weight)
    gate = call(
        functools.partial(gate_kernel, pieces=pieces, share=share, width=width),
        shape_of((pieces, width, share), F32),
        [pltpu.VMEM((share + HALO, width), F32)],
        grid=(1,),
        in_specs=[SCALAR, full_spec((pieces, tokens + HALO, width))]
        + [full_spec((1, model, width))] * pieces
        + [full_spec((KSHORT, 1, width))] * pieces,
        out_specs=full_spec((pieces, width, share)),
    )(me, normed, by_role, *gate_weights[1:], *gate_taps)

    places = pieces if share % LANES == 0 else 1
    convolved = call(
        functools.partial(
            convolve_kernel, length=length, own=own, group=group, padded=padded, tokens=tokens, places=places
        ),
        shape_of((places * groups, own, tokens // places), BF16),
        [pltpu.VMEM((own * rows, LANES), F32), pltpu.VMEM((own * rows, LANES), F32)],
    )(
        regrouped, spectrum, own_bias, tables["forward2"], tables["inverse3"],
        tables["turn_cos"], tables["turn_sin"], tables["mid"], tables["back"],
    )
    if places != pieces:
        convolved = jnp.transpose(convolved.reshape(groups, own, pieces, share), (2, 0, 1, 3))
        convolved = convolved.reshape(pieces * groups, own, share)
    returned = lax.all_to_all(convolved, ("chan", "seq"), split_axis=0, concat_axis=0, tiled=True)
    returned = returned.reshape(pieces, width, share)

    hidden = up_weight.shape[1]
    block = min(512, hidden)
    steps = hidden // block
    results = call(
        functools.partial(tail_kernel, pieces=pieces, share=share, width=width, steps=steps),
        shape_of((pieces, share, width), BF16),
        [pltpu.VMEM((share, model), F32), pltpu.VMEM((share, model), BF16)],
        grid=(steps,),
        in_specs=[
            SCALAR,
            full_spec((pieces, width, share)),
            full_spec((pieces, width, share)),
            full_spec((1, model)),
        ]
        + [full_spec((tokens, width))] * pieces
        + [full_spec((width, model))] * pieces
        + [pl.BlockSpec((model, block), lambda i: (0, i))] * pieces
        + [pl.BlockSpec((block, model), lambda i: (i, 0))] * pieces,
        out_specs=full_spec((pieces, share, width)),
    )(
        me, returned, gate, gain_second[None, :], *x_pieces, *mix_weights, *up_weights, *down_weights,
    )
    received = [results[0]] + [
        lax.ppermute(results[p], "chan", [(i, (i + p) % pieces) for i in range(pieces)])
        for p in range(1, pieces)
    ]
    if pieces == 2:
        first = chan_place == 0
        return jnp.concatenate(
            [jnp.where(first, received[0], received[1]), jnp.where(first, received[1], received[0])], 0
        )
    block_out = jnp.zeros((tokens, width), BF16)
    for p in range(pieces):
        start = lax.rem(chan_place + pieces - p, pieces) * share
        block_out = lax.dynamic_update_slice_in_dim(block_out, received[p], start, 0)
    return block_out


def solution(mesh):
    placed = (
        P("seq", "chan"),
        P(),
        P(None, None, "chan"),
        P(None, None, "chan"),
        P(),
        P(),
        P(),
        P(None, "chan"),
        P("chan"),
        P("chan"),
        P("chan", None),
        P(),
        P(None, "chan"),
        P("chan", None),
    )
    return jax.shard_map(
        per_device, mesh=mesh, in_specs=placed, out_specs=P("seq", "chan"), check_vma=False
    )
```

```python
import functools

import jax
import jax.numpy as jnp
import ml_dtypes
import numpy as np
from jax import lax
from jax.experimental import pallas as pl
from jax.experimental.pallas import tpu as pltpu
from jax.sharding import PartitionSpec as P

BANDS = 12
KSHORT = 3
LANES = 128
HALO = 16
AHEAD = 5
EPS = 1e-05
PI_HIGH = 3.140625
PI_LOW = 9.67653589793e-4
F32 = jnp.float32
BF16 = jnp.bfloat16
VMEM_BYTES = 60 * 1024 * 1024


def matmul(left, right):
    return jnp.dot(left, right, preferred_element_type=F32)


def split_parts(values):
    high = values.astype(BF16)
    return high, (values - high.astype(F32)).astype(BF16)


def split_table(table):
    high = table.astype(np.float32).astype(ml_dtypes.bfloat16)
    low = (table - high.astype(np.float64)).astype(np.float32).astype(ml_dtypes.bfloat16)
    return high, low


def transform_tables(length):
    rows = length // LANES
    period = 2 * rows
    full = 2 * length
    kept = rows + 1
    padded = -(-kept // 8) * 8
    k2 = np.arange(padded)
    valid = (k2 < kept).astype(np.float64)[:, None]
    n2 = np.arange(rows)
    n1 = np.arange(LANES)
    first = 2 * np.pi / period * (k2[:, None] * n2[None, :] % period)
    forward = np.concatenate([np.cos(first) * valid, -np.sin(first) * valid], 0)
    weight = np.where((k2 == 0) | (k2 == rows), 1.0, 2.0)[:, None] * valid
    inverse = np.concatenate([np.cos(first) * weight, -np.sin(first) * weight], 0).T
    turn = 2 * np.pi / full * (k2[:, None] * n1[None, :] % full)
    second = 2 * np.pi / LANES * (n1[:, None] * n1[None, :] % LANES)
    cos2, sin2 = np.cos(second), np.sin(second)
    mid = np.concatenate(
        [np.concatenate([cos2, -sin2], 1), np.concatenate([sin2, cos2], 1)], 0
    )
    back = np.concatenate(
        [np.concatenate([cos2, sin2], 1), np.concatenate([-sin2, cos2], 1)], 0
    ) / full
    f_high, f_low = split_table(forward)
    i_high, i_low = split_table(inverse)
    parts = [np.cos(turn), np.sin(turn)]
    parts = [np.tile(part, (1, 2)).astype(np.float32) for part in parts]
    for table in (mid, back, forward, inverse.T):
        for part in split_table(table):
            wide = np.zeros((part.shape[0], 2 * LANES), np.float32)
            wide[:, : part.shape[1]] = part.astype(np.float32)
            parts.append(wide)
    return np.concatenate(parts, 0), padded


class Packed:
    def __init__(self, own, padded, rows):
        self.padded, self.rows = padded, rows
        sizes = {
            "spectrum": own * padded, "cos": padded, "sin": padded,
            "mid_high": 2 * LANES, "mid_low": 2 * LANES, "back_high": 2 * LANES, "back_low": 2 * LANES,
            "forward_high": 2 * padded, "forward_low": 2 * padded,
            "inverse_high": 2 * padded, "inverse_low": 2 * padded,
            "direct": -(-own // 8) * 8,
        }
        self.start, self.size, place = {}, sizes, 0
        for name, size in sizes.items():
            self.start[name] = place
            place += size
        self.total = place

    def get(self, ref, name, lanes=2 * LANES, base=0):
        start = self.start[name] - base
        return ref[start : start + self.size[name], :lanes]

    def half(self, ref, name, lanes=2 * LANES, base=0):
        return self.get(ref, name, lanes, base).astype(BF16)


def sine(values):
    count = jnp.floor(values * (1.0 / np.pi) + 0.5)
    rest = (values - count * PI_HIGH) - count * PI_LOW
    half = count * 0.5
    sign = 1.0 - 4.0 * (half - jnp.floor(half))
    return sign * sine_poly(rest)


def sine_poly(rest):
    square = rest * rest
    poly = -2.5052108385441720e-08
    poly = poly * square + 2.7557319223985893e-06
    poly = poly * square - 1.9841269841269841e-04
    poly = poly * square + 8.3333333333333333e-03
    poly = poly * square - 1.6666666666666667e-01
    return rest + rest * square * poly


def sine_turns(turns):
    count = jnp.floor(turns * 2.0 + 0.5)
    rest = (turns - count * 0.5) * (2.0 * np.pi)
    half = count * 0.5
    sign = 1.0 - 4.0 * (half - jnp.floor(half))
    return sign * sine_poly(rest)


def rows_to_spectrum(load_pair, group, table, turn_cos, turn_sin, mid_high, mid_low, padded):
    stacked = []
    for pair in range(group // 2):
        first = matmul(table, load_pair(pair))
        real, imag = first[:padded], first[padded:]
        turned_real = real * turn_cos + imag * turn_sin
        turned_imag = imag * turn_cos - real * turn_sin
        for side in range(2):
            lanes = slice(side * LANES, (side + 1) * LANES)
            stacked.append(jnp.concatenate([turned_real[:, lanes], turned_imag[:, lanes]], 1))
    high, low = split_parts(jnp.concatenate(stacked, 0))
    return matmul(high, mid_high) + matmul(low, mid_high) + matmul(high, mid_low)


def project_kernel(
    place_ref, *refs, pieces, tokens, width, own, own_rows, share
):
    x_refs, refs = refs[:pieces], refs[pieces:]
    gain_ref, taps_ref, w_hbm, normed_hbm, edge_ref, rows_ref, out_hbm, refs = *refs[:7], refs[7:]
    w_ref, proj_ref, block_ref, normed_ref, w_sems, out_sems, normed_sem = refs
    me = place_ref[0]
    places = [lax.rem(me + p, pieces) for p in range(pieces)]
    total = pieces * width
    loads = [pltpu.make_async_copy(w_hbm.at[role + 1], w_ref.at[role], w_sems.at[role]) for role in range(2)]
    for load in loads:
        load.start()
    chunk = 128
    for start in range(0, tokens, chunk):
        values = [ref[start : start + chunk, :].astype(F32) for ref in x_refs]
        mean = sum(jnp.sum(v, axis=1, keepdims=True) for v in values) / total
        centered = [v - mean for v in values]
        spread = sum(jnp.sum(c * c, axis=1, keepdims=True) for c in centered) / total
        scale = lax.rsqrt(spread + EPS)
        for p in range(pieces):
            gain = gain_ref[places[p]]
            normed_ref[p, start : start + chunk, :] = (centered[p] * scale * gain).astype(BF16)
    mine = pl.ds(pl.multiple_of(me * share, 16), share)
    for p in range(pieces):
        edge_ref[p] = normed_ref[p, tokens - HALO :, :]
        rows_ref[p] = x_refs[p][mine, :]
    keep = pltpu.make_async_copy(normed_ref, normed_hbm, normed_sem)
    keep.start()
    step = min(width, 256)
    per_step = step // own
    parts = tokens // LANES
    proj_ref[:, :8, :] = jnp.zeros((2, 8, step), F32)
    for load in loads:
        load.wait()
    stores = []
    for col in range(0, width, step):
        cols = slice(col, col + step)
        for role in range(2):
            sums = 0.0
            for p in range(pieces):
                rows = pl.ds(pl.multiple_of(places[p] * width, width), width)
                sums = sums + matmul(normed_ref[p], w_ref[role, rows, cols])
            proj_ref[role, 8:, :] = sums.astype(BF16).astype(F32)
        shorted = []
        for role in range(2):
            value = taps_ref[0, role + 1 : role + 2, cols] * proj_ref[role, 8 : 8 + tokens, :]
            for lag in range(1, KSHORT):
                value = (
                    value
                    + taps_ref[lag, role + 1 : role + 2, cols] * proj_ref[role, 8 - lag : 8 - lag + tokens, :]
                )
            shorted.append(value)
        gated = (shorted[1] * shorted[0]).T
        edges = jnp.concatenate(
            [
                proj_ref[0, 8:10, :],
                proj_ref[0, 6 + tokens : 8 + tokens, :],
                proj_ref[1, 8:10, :],
                proj_ref[1, 6 + tokens : 8 + tokens, :],
                jnp.zeros((8, step), F32),
            ],
            0,
        )
        first = col // own
        for d in range(per_step):
            for part in range(parts):
                block_ref[first + d, part * own_rows : part * own_rows + own, :] = gated[
                    d * own : (d + 1) * own, part * LANES : (part + 1) * LANES
                ].astype(BF16)
            block_ref[first + d, parts * own_rows :, :] = jnp.concatenate(
                [edges[:, d * own : (d + 1) * own], jnp.zeros((16, LANES - own), F32)], 1
            ).astype(BF16)
        targets = pl.ds(first, per_step)
        store = pltpu.make_async_copy(block_ref.at[targets], out_hbm.at[targets], out_sems.at[col // step])
        store.start()
        stores.append(store)
    for store in stores:
        store.wait()
    keep.wait()


def gate_kernel(place_ref, normed_ref, halo_ref, *refs, pieces, share, width):
    tap_refs, refs = refs[:pieces], refs[pieces:]
    w_hbm, (gate_ref, w_ref, rows_ref, proj_ref, w_sems) = refs[:pieces], refs[pieces:]
    loads = [pltpu.make_async_copy(w_hbm[p].at[0], w_ref.at[p], w_sems.at[p]) for p in range(pieces)]
    for load in loads:
        load.start()
    me = place_ref[0]
    places = [lax.rem(me + p, pieces) for p in range(pieces)]
    mine = pl.ds(pl.multiple_of(me * share, 16), share)
    before = pl.ds(pl.multiple_of(jnp.maximum(me * share - HALO, 0), 16), HALO)
    for p in range(pieces):
        rows_ref[p, HALO:, :] = normed_ref[p, mine, :]
        rows_ref[p, :HALO, :] = jnp.where(
            me == 0, halo_ref[p].astype(F32), normed_ref[p, before, :].astype(F32)
        ).astype(BF16)
    for load in loads:
        load.wait()
    for out in range(pieces):
        sums = 0.0
        for p in range(pieces):
            rows = pl.ds(pl.multiple_of(places[p] * width, width), width)
            sums = sums + matmul(rows_ref[p], w_ref[out, rows, :])
        proj_ref[...] = sums.astype(BF16).astype(F32)
        value = tap_refs[out][0, 0:1, :] * proj_ref[HALO : HALO + share, :]
        for lag in range(1, KSHORT):
            value = value + tap_refs[out][lag, 0:1, :] * proj_ref[HALO - lag : HALO - lag + share, :]
        gate_ref[out] = value.T


def filter_kernel(
    place_ref, in_ref, bias_ref, mid_w_ref, out_w_ref, decay_ref, direct_ref, taps_ref,
    tables_ref, packed_ref, own_taps_ref, response_ref, columns_ref, scalars_ref, in_pad_ref, *, length, own, group, packed
):
    padded = packed.padded
    seq_place = place_ref[1]
    width = out_w_ref.shape[1]
    base = packed.start["cos"]
    packed_ref[base : base + tables_ref.shape[0], :] = tables_ref[...]
    feats = in_pad_ref.shape[0]
    in_pad_ref[...] = jnp.zeros(in_pad_ref.shape, F32)
    in_pad_ref[: in_ref.shape[0], :] = in_ref[...].astype(F32)
    in_columns = in_pad_ref[...].T.astype(BF16)
    mid_columns = mid_w_ref[...].astype(F32).T.astype(BF16)
    bias = jnp.broadcast_to(bias_ref[...], (8, bias_ref.shape[1])).T[:, :1]
    columns_ref[...] = out_w_ref[...].astype(F32).T
    scalars_ref[...] = jnp.concatenate(
        [jnp.broadcast_to(decay_ref[...], (4, width)), jnp.broadcast_to(direct_ref[...], (4, width))], 0
    ).T
    mine = pl.ds(seq_place * own, own)
    out_columns = columns_ref[mine, :].astype(BF16)
    decay = scalars_ref[mine, 0:1]
    at = packed.start["direct"]
    packed_ref[at : at + own, :] = jnp.broadcast_to(scalars_ref[mine, 4:5], (own, 2 * LANES))
    shift = lax.rem(width - seq_place * own, width)
    for lag in range(KSHORT):
        own_taps = pltpu.roll(jnp.concatenate([taps_ref[lag], jnp.zeros((5, width), F32)], 0), shift, 1)
        own_taps_ref[lag] = own_taps[:, :LANES]
    rows = length // LANES
    chunk = min(1024, length)
    row_ids = lax.broadcasted_iota(jnp.int32, (feats, chunk), 0)
    band = jnp.where(row_ids > BANDS, row_ids - (BANDS + 1), row_ids - 1)
    band = jnp.clip(band, 0, BANDS - 1)
    quarter = jnp.where(row_ids <= BANDS, 0.25, 0.0)
    for start in range(0, length, chunk):
        places = lax.broadcasted_iota(jnp.int32, (feats, chunk), 1) + start
        phase = lax.shift_left(places, band) & (length - 1)
        turns = phase.astype(F32) * (1.0 / length)
        waves = sine_turns(turns + quarter)
        features = jnp.where(
            row_ids == 0,
            places.astype(F32) / length,
            jnp.where(row_ids <= 2 * BANDS, waves, 0.0),
        ).astype(BF16)
        first = sine(matmul(in_columns, features) + bias).astype(BF16)
        second = sine(matmul(mid_columns, first)).astype(BF16)
        ramp = (lax.broadcasted_iota(jnp.int32, (1, chunk), 1) + start).astype(F32) / length
        response = matmul(out_columns, second) * jnp.exp(-decay * ramp)
        for part in range(chunk // LANES):
            row = start // LANES + part
            response_ref[pl.ds(row, own, stride=rows), :] = response[:, part * LANES : (part + 1) * LANES]

    high = packed.half(tables_ref, "forward_high", rows, base)
    table = jnp.concatenate([high, high, packed.half(tables_ref, "forward_low", rows, base)], 1)
    turn_cos, turn_sin = packed.get(tables_ref, "cos", base=base), packed.get(tables_ref, "sin", base=base)
    mid_high, mid_low = packed.half(tables_ref, "mid_high", base=base), packed.half(tables_ref, "mid_low", base=base)

    def one_group(step, carry):
        def load_pair(pair):
            base = (step * group + 2 * pair) * rows
            both = [
                response_ref[pl.ds(pl.multiple_of(base + side * rows, 8), rows), :] for side in range(2)
            ]
            high, low = split_parts(jnp.concatenate(both, 1))
            return jnp.concatenate([high, low, high], 0)

        spectrum = rows_to_spectrum(
            load_pair, group, table, turn_cos, turn_sin, mid_high, mid_low, padded
        )
        packed_ref[pl.ds(pl.multiple_of(step * group * padded, 8), group * padded), :] = spectrum
        return carry

    lax.fori_loop(0, own // group, one_group, 0)


def convolve_kernel(
    x_ref, taps_ref, packed_hbm, out_ref, signal_ref, result_ref, packed_ref, sem,
    *, length, own, own_rows, group, packed, tokens, places
):
    padded = packed.padded
    load = pltpu.make_async_copy(packed_hbm, packed_ref, sem)
    load.start()
    rows = length // LANES
    per_block = tokens // LANES
    blocks = length // tokens
    lane = lax.broadcasted_iota(jnp.int32, (own, LANES), 1)
    fixes = []
    last = [jnp.zeros((2, LANES), F32)] * 2
    for block in range(blocks):
        edge = x_ref[block, per_block * own_rows :, :].astype(F32)
        starts = []
        for role in range(2):
            here, before = edge[4 * role : 4 * role + 2], last[role]
            two_back = jnp.concatenate([before[1:2], here[0:1]], 0)
            starts.append(
                taps_ref[0, role + 1 : role + 2, :] * here
                + taps_ref[1, role + 1 : role + 2, :] * two_back
                + taps_ref[2, role + 1 : role + 2, :] * before
            )
            last[role] = edge[4 * role + 2 : 4 * role + 4]
        fixes.append(starts[1] * starts[0])
    fixed = jnp.concatenate(fixes, 0)
    if 2 * blocks < LANES:
        fixed = jnp.concatenate([fixed, jnp.zeros((LANES - 2 * blocks, LANES), F32)], 0)
    fixed = fixed.T[:own]
    for row in range(rows):
        block, part = divmod(row, per_block)
        values = x_ref[block, part * own_rows : part * own_rows + own, :].astype(F32)
        if part == 0:
            values = jnp.where(lane == 0, fixed[:, 2 * block : 2 * block + 1], values)
            values = jnp.where(lane == 1, fixed[:, 2 * block + 1 : 2 * block + 2], values)
        signal_ref[pl.ds(row, own, stride=rows), :] = values
    load.wait()
    turn_cos, turn_sin = packed.get(packed_ref, "cos"), packed.get(packed_ref, "sin")
    mid_high, mid_low = packed.half(packed_ref, "mid_high"), packed.half(packed_ref, "mid_low")
    back_high, back_low = packed.half(packed_ref, "back_high"), packed.half(packed_ref, "back_low")
    table = jnp.concatenate(
        [packed.half(packed_ref, "forward_high", rows), packed.half(packed_ref, "forward_low", rows)], 1
    )
    inverse = packed.get(packed_ref, "inverse_high", rows).T.astype(BF16)
    inverse = jnp.concatenate([inverse, inverse, packed.get(packed_ref, "inverse_low", rows).T.astype(BF16)], 1)

    def one_group(step, carry):
        def load_pair(pair):
            base = (step * group + 2 * pair) * rows
            both = [
                signal_ref[pl.ds(pl.multiple_of(base + side * rows, 8), rows), :] for side in range(2)
            ]
            values = jnp.concatenate(both, 1).astype(BF16)
            return jnp.concatenate([values, values], 0)

        signal = rows_to_spectrum(load_pair, group, table, turn_cos, turn_sin, mid_high, mid_low, padded)
        other = packed_ref[pl.ds(pl.multiple_of(step * group * padded, 8), group * padded), :]
        s_real, s_imag = signal[:, :LANES], signal[:, LANES:]
        f_real, f_imag = other[:, :LANES], other[:, LANES:]
        product = jnp.concatenate(
            [s_real * f_real - s_imag * f_imag, s_real * f_imag + s_imag * f_real], 1
        )
        high, low = split_parts(product)
        mixed = matmul(high, back_high) + matmul(low, back_high) + matmul(high, back_low)
        for pair in range(group // 2):
            first = mixed[2 * pair * padded : (2 * pair + 1) * padded]
            second = mixed[(2 * pair + 1) * padded : (2 * pair + 2) * padded]
            real = jnp.concatenate([first[:, :LANES], second[:, :LANES]], 1)
            imag = jnp.concatenate([first[:, LANES:], second[:, LANES:]], 1)
            turned = jnp.concatenate(
                [real * turn_cos - imag * turn_sin, imag * turn_cos + real * turn_sin], 0
            )
            t_high, t_low = split_parts(turned)
            values = matmul(inverse, jnp.concatenate([t_high, t_low, t_high], 0))
            base = (step * group + 2 * pair) * rows
            for side in range(2):
                result_ref[pl.ds(pl.multiple_of(base + side * rows, 8), rows), :] = values[
                    :, side * LANES : (side + 1) * LANES
                ]
        return carry

    lax.fori_loop(0, own // group, one_group, 0)
    bias = packed.get(packed_ref, "direct", LANES)[:own]
    share_rows = per_block // places
    for row in range(rows):
        block, part = divmod(row, per_block)
        place, side = divmod(part, share_rows)
        values = result_ref[pl.ds(row, own, stride=rows), :]
        values = values + bias * signal_ref[pl.ds(row, own, stride=rows), :]
        target = place * (rows // per_block) + block
        out_ref[target, :, side * LANES : (side + 1) * LANES] = values.astype(BF16)


def gelu(values):
    return values * (lax.erf(values * np.float32(0.5**0.5)) + 1.0) * 0.5


def tail_kernel(place_ref, z_ref, gate_ref, gain_ref, rows_ref, *refs, pieces, share, width, block):
    mix_hbm, refs = refs[:pieces], refs[pieces:]
    up_hbm, refs = refs[:pieces], refs[pieces:]
    down_hbm, refs = refs[:pieces], refs[pieces:]
    out_refs, refs = refs[:pieces], refs[pieces:]
    sums_ref, hidden_ref, mix_ref, up_ref, down_ref, mix_sems, up_sems, down_sems = refs
    total = pieces * width
    units = hidden_ref.shape[2]
    steps = units // block
    copies = []
    for p in range(pieces):
        copies.append(pltpu.make_async_copy(mix_hbm[p], mix_ref.at[p], mix_sems.at[p]))
    for p in range(pieces):
        for k in range(steps):
            cols = pl.ds(k * block, block)
            copies.append(pltpu.make_async_copy(up_hbm[p].at[:, cols], up_ref.at[p, :, cols], up_sems.at[p, k]))
    for p in range(pieces):
        for k in range(steps):
            cols = pl.ds(k * block, block)
            copies.append(pltpu.make_async_copy(down_hbm[p].at[cols], down_ref.at[p, cols], down_sems.at[p, k]))
    started, waited = [0], [0]

    def start_until(count):
        while started[0] < min(count, len(copies)):
            copies[started[0]].start()
            started[0] += 1

    def next_copy():
        start_until(waited[0] + AHEAD)
        copies[waited[0]].wait()
        waited[0] += 1

    start_until(AHEAD)
    me = place_ref[0]
    places = [lax.rem(me + p, pieces) for p in range(pieces)]
    dims = (((0,), (0,)), ((), ()))
    mixed = [(z_ref[places[p]].astype(F32) * gate_ref[p]).astype(BF16) for p in range(pieces)]
    sums = 0.0
    for p in range(pieces):
        next_copy()
        sums = sums + lax.dot_general(mixed[p], mix_ref[p], dims, preferred_element_type=F32)
    sums_ref[...] = sums
    for p in range(pieces):
        cols = pl.ds(pl.multiple_of(places[p] * width, LANES), width)
        residual = rows_ref[p].astype(F32) + sums_ref[:, cols]
        sums_ref[:, cols] = residual.astype(BF16).astype(F32)
    values = sums_ref[...]
    mean = jnp.sum(values, axis=1, keepdims=True) / total
    centered = values - mean
    spread = jnp.sum(centered * centered, axis=1, keepdims=True) / total
    normed = (centered * lax.rsqrt(spread + EPS) * gain_ref[...]).astype(BF16)
    for p in range(pieces):
        for k in range(steps):
            next_copy()
            cols = slice(k * block, (k + 1) * block)
            hidden_ref[p, :, cols] = gelu(matmul(normed, up_ref[p, :, cols])).astype(BF16)
    sums = sums_ref[...]
    for p in range(pieces):
        for k in range(steps):
            next_copy()
        sums = sums + matmul(hidden_ref[p], down_ref[p])
    sums_ref[...] = sums
    for p in range(pieces):
        cols = pl.ds(pl.multiple_of(places[p] * width, LANES), width)
        out_refs[p][...] = sums_ref[:, cols].astype(BF16)


def join_kernel(place_ref, *refs, pieces, share):
    out_ref = refs[pieces]
    me = place_ref[0]
    for p in range(pieces):
        start = lax.rem(me + pieces - p, pieces) * share
        out_ref[pl.ds(pl.multiple_of(start, 16), share), :] = refs[p][...]


HBM = pl.BlockSpec(memory_space=pltpu.HBM)
VMEM = pl.BlockSpec(memory_space=pltpu.VMEM)
SMEM = pl.BlockSpec(memory_space=pltpu.SMEM)


def call(kernel, in_specs, out_specs, out_shape, scratch, megabytes, *args):
    kinds = {"s": SMEM, "h": HBM, "v": VMEM, "c": VMEM}
    spaces = {"h": pltpu.HBM, "v": pltpu.VMEM, "c": pltpu.HBM}
    placed = [
        pltpu.with_memory_space_constraint(arg, spaces[kind]) if kind in spaces else arg
        for kind, arg in zip(in_specs, args, strict=True)
    ]
    return pl.pallas_call(
        kernel,
        in_specs=[kinds[kind] for kind in in_specs],
        out_specs=out_specs,
        out_shape=out_shape,
        scratch_shapes=scratch,
        compiler_params=pltpu.CompilerParams(vmem_limit_bytes=megabytes * 1024 * 1024),
    )(*placed)


def shape_of(shape, dtype):
    return jax.ShapeDtypeStruct(shape, dtype)


def per_device(
    layer_input, gain_first, in_weight, short_weight, filt_in, filt_bias, filt_mid, filt_out,
    decay_rate, conv_bias, out_weight, gain_second, up_weight, down_weight,
):
    tokens, width = layer_input.shape
    pieces = lax.axis_size("chan")
    groups = lax.axis_size("seq")
    chan_place = lax.axis_index("chan")
    model = pieces * width
    length = tokens * groups
    share = tokens // pieces
    own = width // groups
    own_rows = -(-own // 16) * 16
    block_rows = tokens // LANES * own_rows + 16
    place = jnp.stack([chan_place, lax.axis_index("seq")]).astype(jnp.int32)

    def turned(array, by):
        if by == 0:
            return array
        return lax.ppermute(array, "chan", [(i, (i - by) % pieces) for i in range(pieces)])

    def all_turned(array):
        return [turned(array, p) for p in range(pieces)]

    x_pieces = all_turned(layer_input)
    by_role = jnp.transpose(in_weight, (1, 0, 2))
    step = min(width, 256)
    normed, edges, my_rows, gated = call(
        functools.partial(
            project_kernel, pieces=pieces, tokens=tokens, width=width, own=own, own_rows=own_rows, share=share
        ),
        "sc" + "v" * (pieces - 1) + "cch",
        (HBM, VMEM, VMEM, HBM),
        (
            pltpu.HBM((pieces, tokens, width), BF16),
            shape_of((pieces, HALO, width), BF16),
            pltpu.VMEM((pieces, share, width), BF16),
            pltpu.HBM((groups, block_rows, LANES), BF16),
        ),
        [
            pltpu.VMEM((2, model, width), BF16),
            pltpu.VMEM((2, tokens + 8, step), F32),
            pltpu.VMEM((groups, block_rows, LANES), BF16),
            pltpu.VMEM((pieces, tokens, width), BF16),
            pltpu.SemaphoreType.DMA((2,)),
            pltpu.SemaphoreType.DMA((width // step,)),
            pltpu.SemaphoreType.DMA,
        ],
        20,
        place, *x_pieces, gain_first.reshape(pieces, 1, width), short_weight, by_role,
    )
    by_role, out_weight, up_weight, down_weight, gated = lax.optimization_barrier(
        (by_role, out_weight, up_weight, down_weight, gated)
    )
    regrouped = lax.all_to_all(gated, "seq", split_axis=0, concat_axis=0, tiled=True)

    tables, padded = transform_tables(length)
    rows = length // LANES
    packed = Packed(own, padded, rows)
    group = min(8, own)
    filters = filt_mid.shape[0]
    spectrum, own_taps = call(
        functools.partial(filter_kernel, length=length, own=own, group=group, packed=packed),
        "s" + "c" * 8,
        (VMEM, VMEM),
        (pltpu.HBM((packed.total, 2 * LANES), F32), pltpu.VMEM((KSHORT, 8, LANES), F32)),
        [
            pltpu.VMEM((own * rows, LANES), F32),
            pltpu.VMEM((width, filters), F32),
            pltpu.VMEM((width, 8), F32),
            pltpu.VMEM((32, filters), F32),
        ],
        24,
        place, filt_in, filt_bias[None, :], filt_mid, filt_out, decay_rate[None, :], conv_bias[None, :],
        short_weight, jnp.asarray(tables),
    )
    places = pieces if share % LANES == 0 else 1
    convolved = call(
        functools.partial(
            convolve_kernel, length=length, own=own, own_rows=own_rows, group=group, packed=packed,
            tokens=tokens, places=places,
        ),
        "vvh",
        VMEM,
        pltpu.HBM((places * groups, own, tokens // places), BF16),
        [
            pltpu.VMEM((own * rows, LANES), F32),
            pltpu.VMEM((own * rows, LANES), F32),
            pltpu.VMEM((packed.total, 2 * LANES), F32),
            pltpu.SemaphoreType.DMA,
        ],
        24,
        regrouped, own_taps, spectrum,
    )
    edges, late_place, convolved = lax.optimization_barrier((edges, place, convolved))
    if places != pieces:
        convolved = jnp.transpose(convolved.reshape(groups, own, pieces, share), (2, 0, 1, 3))
        convolved = convolved.reshape(pieces * groups, own, share)
    returned = lax.all_to_all(convolved, ("chan", "seq"), split_axis=0, concat_axis=0, tiled=True)
    returned = returned.reshape(pieces, width, share)

    halo = lax.ppermute(edges, "seq", [(i, i + 1) for i in range(groups - 1)])
    mix_weights = all_turned(out_weight)
    up_weights = all_turned(up_weight)
    down_weights = all_turned(down_weight)
    big = [*mix_weights, *up_weights, *down_weights]
    gate = call(
        functools.partial(gate_kernel, pieces=pieces, share=share, width=width),
        "scvc" + "v" * (pieces - 1) + "h" * pieces,
        VMEM,
        pltpu.VMEM((pieces, width, share), F32),
        [
            pltpu.VMEM((pieces, model, width), BF16),
            pltpu.VMEM((pieces, share + HALO, width), BF16),
            pltpu.VMEM((share + HALO, width), F32),
            pltpu.SemaphoreType.DMA((pieces,)),
        ],
        16,
        late_place, normed, halo, *all_turned(short_weight), *all_turned(by_role),
    )
    units = up_weight.shape[1]
    block = min(512, units)
    results = call(
        functools.partial(tail_kernel, pieces=pieces, share=share, width=width, block=block),
        "svvcv" + "h" * (3 * pieces),
        (VMEM,) * pieces,
        tuple(shape_of((share, width), BF16) for p in range(pieces)),
        [
            pltpu.VMEM((share, model), F32),
            pltpu.VMEM((pieces, share, units), BF16),
            pltpu.VMEM((pieces, width, model), BF16),
            pltpu.VMEM((pieces, model, units), BF16),
            pltpu.VMEM((pieces, units, model), BF16),
            pltpu.SemaphoreType.DMA((pieces,)),
            pltpu.SemaphoreType.DMA((pieces, units // block)),
            pltpu.SemaphoreType.DMA((pieces, units // block)),
        ],
        44,
        place, returned, gate, gain_second[None, :], my_rows, *big,
    )
    received = [results[0]] + [
        lax.ppermute(results[p], "chan", [(i, (i + p) % pieces) for i in range(pieces)])
        for p in range(1, pieces)
    ]
    return call(
        functools.partial(join_kernel, pieces=pieces, share=share),
        "s" + "v" * pieces,
        VMEM,
        shape_of((tokens, width), BF16),
        [],
        8,
        place, *received,
    )


def solution(mesh):
    placed = (
        P("seq", "chan"),
        P(),
        P(None, None, "chan"),
        P(None, None, "chan"),
        P(),
        P(),
        P(),
        P(None, "chan"),
        P("chan"),
        P("chan"),
        P("chan", None),
        P(),
        P(None, "chan"),
        P("chan", None),
    )
    return jax.shard_map(
        per_device, mesh=mesh, in_specs=placed, out_specs=P("seq", "chan"), check_vma=False
    )
```

```python
import functools

import jax
import jax.numpy as jnp
import ml_dtypes
import numpy as np
from jax import lax
from jax.experimental import pallas as pl
from jax.experimental.pallas import tpu as pltpu
from jax.sharding import PartitionSpec as P

BANDS = 12
KSHORT = 3
LANES = 128
HALO = 16
AHEAD = 6
EPS = 1e-05
PI_HIGH = 3.140625
PI_LOW = 9.67653589793e-4
F32 = jnp.float32
BF16 = jnp.bfloat16
VMEM_BYTES = 60 * 1024 * 1024


def matmul(left, right):
    return jnp.dot(left, right, preferred_element_type=F32)


def split_parts(values):
    high = values.astype(BF16)
    return high, (values - high.astype(F32)).astype(BF16)


def split_table(table):
    high = table.astype(np.float32).astype(ml_dtypes.bfloat16)
    low = (table - high.astype(np.float64)).astype(np.float32).astype(ml_dtypes.bfloat16)
    return high, low


def transform_tables(length):
    rows = length // LANES
    period = 2 * rows
    full = 2 * length
    kept = rows + 1
    padded = -(-kept // 8) * 8
    k2 = np.arange(padded)
    valid = (k2 < kept).astype(np.float64)[:, None]
    n2 = np.arange(rows)
    n1 = np.arange(LANES)
    first = 2 * np.pi / period * (k2[:, None] * n2[None, :] % period)
    forward = np.concatenate([np.cos(first) * valid, -np.sin(first) * valid], 0)
    weight = np.where((k2 == 0) | (k2 == rows), 1.0, 2.0)[:, None] * valid
    inverse = np.concatenate([np.cos(first) * weight, -np.sin(first) * weight], 0).T
    turn = 2 * np.pi / full * (k2[:, None] * n1[None, :] % full)
    second = 2 * np.pi / LANES * (n1[:, None] * n1[None, :] % LANES)
    cos2, sin2 = np.cos(second), np.sin(second)
    mid = np.concatenate(
        [np.concatenate([cos2, -sin2], 1), np.concatenate([sin2, cos2], 1)], 0
    )
    back = np.concatenate(
        [np.concatenate([cos2, sin2], 1), np.concatenate([-sin2, cos2], 1)], 0
    ) / full
    f_high, f_low = split_table(forward)
    i_high, i_low = split_table(inverse)
    f_high, f_low = split_table(forward)
    i_high, i_low = split_table(inverse)
    return {
        "turn": np.tile(np.stack([np.cos(turn), np.sin(turn)]), (1, 1, 2)).astype(np.float32),
        "square": np.stack([*split_table(mid), *split_table(back)]),
        "forward3": np.concatenate([f_high, f_high, f_low], 1),
        "forward2": np.concatenate([f_high, f_low], 1),
        "inverse3": np.concatenate([i_high, i_high, i_low], 1),
    }


def sine(values):
    count = jnp.floor(values * (1.0 / np.pi) + 0.5)
    rest = (values - count * PI_HIGH) - count * PI_LOW
    half = count * 0.5
    sign = 1.0 - 4.0 * (half - jnp.floor(half))
    return sign * sine_poly(rest)


def sine_poly(rest):
    square = rest * rest
    poly = -2.5052108385441720e-08
    poly = poly * square + 2.7557319223985893e-06
    poly = poly * square - 1.9841269841269841e-04
    poly = poly * square + 8.3333333333333333e-03
    poly = poly * square - 1.6666666666666667e-01
    return rest + rest * square * poly


def sine_turns(turns):
    count = jnp.floor(turns * 2.0 + 0.5)
    rest = (turns - count * 0.5) * (2.0 * np.pi)
    half = count * 0.5
    sign = 1.0 - 4.0 * (half - jnp.floor(half))
    return sign * sine_poly(rest)


def rows_to_spectrum(load_pair, group, table, turn_cos, turn_sin, mid_high, mid_low, padded):
    stacked = []
    for pair in range(group // 2):
        first = matmul(table, load_pair(pair))
        real, imag = first[:padded], first[padded:]
        turned_real = real * turn_cos + imag * turn_sin
        turned_imag = imag * turn_cos - real * turn_sin
        for side in range(2):
            lanes = slice(side * LANES, (side + 1) * LANES)
            stacked.append(jnp.concatenate([turned_real[:, lanes], turned_imag[:, lanes]], 1))
    high, low = split_parts(jnp.concatenate(stacked, 0))
    return matmul(high, mid_high) + matmul(low, mid_high) + matmul(high, mid_low)


def project_kernel(
    *refs, pieces, tokens, width, own, own_rows, share
):
    x_refs, refs = refs[:pieces], refs[pieces:]
    gain_ref, taps_ref, w_hbm, normed_hbm, rows_hbm, out_hbm, refs = *refs[:6], refs[6:]
    w_ref, proj_ref, block_ref, normed_ref, w_sems, out_sems, normed_sem, row_sems = refs
    me = lax.axis_index("chan")
    places = [lax.rem(me + p, pieces) for p in range(pieces)]
    total = pieces * width
    loads = [pltpu.make_async_copy(w_hbm.at[(role + 1) % 3], w_ref.at[role], w_sems.at[role]) for role in range(3)]
    for load in loads:
        load.start()
    chunk = 128
    for start in range(0, tokens, chunk):
        values = [ref[start : start + chunk, :].astype(F32) for ref in x_refs]
        mean = sum(jnp.sum(v, axis=1, keepdims=True) for v in values) / total
        centered = [v - mean for v in values]
        spread = sum(jnp.sum(c * c, axis=1, keepdims=True) for c in centered) / total
        scale = lax.rsqrt(spread + EPS)
        for p in range(pieces):
            gain = gain_ref[places[p]]
            normed_ref[p, start : start + chunk, :] = (centered[p] * scale * gain).astype(BF16)
    mine = pl.ds(pl.multiple_of(me * share, 16), share)
    keeps = [pltpu.make_async_copy(normed_ref, normed_hbm, normed_sem)]
    for p in range(pieces):
        keeps.append(pltpu.make_async_copy(x_refs[p].at[mine], rows_hbm.at[p], row_sems.at[p]))
    for keep in keeps:
        keep.start()
    step = min(width, 256)
    per_step = step // own
    parts = tokens // LANES
    proj_ref[:, :8, :] = jnp.zeros((2, 8, step), F32)
    for load in loads[:2]:
        load.wait()
    stores = []
    for col in range(0, width, step):
        cols = slice(col, col + step)
        for role in range(2):
            sums = 0.0
            for p in range(pieces):
                rows = pl.ds(pl.multiple_of(places[p] * width, width), width)
                sums = sums + matmul(normed_ref[p], w_ref[role, rows, cols])
            proj_ref[role, 8:, :] = sums.astype(BF16).astype(F32)
        shorted = []
        for role in range(2):
            value = taps_ref[0, role + 1 : role + 2, cols] * proj_ref[role, 8 : 8 + tokens, :]
            for lag in range(1, KSHORT):
                value = (
                    value
                    + taps_ref[lag, role + 1 : role + 2, cols] * proj_ref[role, 8 - lag : 8 - lag + tokens, :]
                )
            shorted.append(value)
        gated = (shorted[1] * shorted[0]).T
        if col == 0:
            loads[2].wait()
            last = 0.0
            for p in range(pieces):
                rows = pl.ds(pl.multiple_of(places[p] * width, width), width)
                last = last + matmul(normed_ref[p, tokens - HALO :, :], w_ref[2, rows, :])
            last = last.astype(BF16).astype(F32)
            spread_last = [
                last[row : row + 1, lane : lane + LANES]
                for row in (HALO - 2, HALO - 1)
                for lane in range(0, width, LANES)
            ]
            spread_last = jnp.concatenate(spread_last + [jnp.zeros((8 - len(spread_last), LANES), F32)][: len(spread_last) < 8], 0)
        edges = jnp.concatenate(
            [
                proj_ref[0, 8:10, :],
                proj_ref[0, 6 + tokens : 8 + tokens, :],
                proj_ref[1, 8:10, :],
                proj_ref[1, 6 + tokens : 8 + tokens, :],
            ],
            0,
        )
        first = col // own
        for d in range(per_step):
            for part in range(parts):
                block_ref[first + d, part * own_rows : part * own_rows + own, :] = gated[
                    d * own : (d + 1) * own, part * LANES : (part + 1) * LANES
                ].astype(BF16)
            block_edges = jnp.concatenate([edges[:, d * own : (d + 1) * own], jnp.zeros((8, LANES - own), F32)], 1)
            block_ref[first + d, parts * own_rows :, :] = jnp.concatenate([block_edges, spread_last], 0).astype(BF16)
        targets = pl.ds(first, per_step)
        store = pltpu.make_async_copy(block_ref.at[targets], out_hbm.at[targets], out_sems.at[col // step])
        store.start()
        stores.append(store)
    for store in stores:
        store.wait()
    for keep in keeps:
        keep.wait()


def gate_kernel(normed_ref, *refs, pieces, share, width, rest):
    side_refs, refs = refs[:pieces], refs[pieces:]
    w_hbm, refs = refs[:pieces], refs[pieces:]
    mix_hbm, (gate_ref, mix_ref, w_ref, rows_ref, proj_ref, w_sems, mix_sems) = refs[:pieces], refs[pieces:]
    fetches = []
    for p in range(pieces):
        size = width - rest if p == pieces - 1 else width
        fetches.append(
            pltpu.make_async_copy(
                mix_hbm[p].at[pl.ds(0, size)], mix_ref.at[pl.ds(p * width, size)], mix_sems.at[p]
            )
        )
    loads = [pltpu.make_async_copy(w_hbm[p].at[0], w_ref.at[p], w_sems.at[p]) for p in range(pieces)]
    for load in loads + fetches:
        load.start()
    me = lax.axis_index("chan")
    places = [lax.rem(me + p, pieces) for p in range(pieces)]
    mine = pl.ds(pl.multiple_of(me * share, 16), share)
    before = pl.ds(pl.multiple_of(jnp.maximum(me * share - HALO, 0), 16), HALO)
    for p in range(pieces):
        rows_ref[p, HALO:, :] = normed_ref[p, mine, :]
        rows_ref[p, :HALO, :] = normed_ref[p, before, :]
    for load in loads:
        load.wait()
    for out in range(pieces):
        sums = 0.0
        for p in range(pieces):
            rows = pl.ds(pl.multiple_of(places[p] * width, width), width)
            sums = sums + matmul(rows_ref[p], w_ref[out, rows, :])
        proj_ref[...] = sums.astype(BF16).astype(F32)
        proj_ref[HALO - 2 : HALO, :] = jnp.where(
            me == 0, side_refs[out][KSHORT : KSHORT + 2, :], proj_ref[HALO - 2 : HALO, :]
        )
        value = side_refs[out][0:1, :] * proj_ref[HALO : HALO + share, :]
        for lag in range(1, KSHORT):
            value = value + side_refs[out][lag : lag + 1, :] * proj_ref[HALO - lag : HALO - lag + share, :]
        gate_ref[out] = value.T
    for fetch in fetches:
        fetch.wait()


def filter_kernel(
    in_ref, bias_ref, mid_w_ref, out_w_ref, decay_ref, direct_ref, taps_ref,
    turn_ref, square_ref, forward_ref, spectrum_ref, own_taps_ref, own_direct_ref, gate_taps_ref,
    response_ref, columns_ref, scalars_ref, in_pad_ref, *, length, own, group
):
    padded = turn_ref.shape[1]
    seq_place = lax.axis_index("seq")
    width = out_w_ref.shape[1]
    feats = in_pad_ref.shape[0]
    in_pad_ref[...] = jnp.zeros(in_pad_ref.shape, F32)
    in_pad_ref[: in_ref.shape[0], :] = in_ref[...].astype(F32)
    in_columns = in_pad_ref[...].T.astype(BF16)
    mid_columns = mid_w_ref[...].astype(F32).T.astype(BF16)
    bias = jnp.broadcast_to(bias_ref[...], (8, bias_ref.shape[1])).T[:, :1]
    columns_ref[...] = out_w_ref[...].astype(F32).T
    scalars_ref[...] = jnp.concatenate(
        [jnp.broadcast_to(decay_ref[...], (4, width)), jnp.broadcast_to(direct_ref[...], (4, width))], 0
    ).T
    mine = pl.ds(seq_place * own, own)
    out_columns = columns_ref[mine, :].astype(BF16)
    decay = scalars_ref[mine, 0:1]
    own_direct_ref[...] = jnp.broadcast_to(scalars_ref[mine, 4:5], (own, LANES))
    shift = lax.rem(width - seq_place * own, width)
    for lag in range(KSHORT):
        own_taps = pltpu.roll(jnp.concatenate([taps_ref[lag], jnp.zeros((5, width), F32)], 0), shift, 1)
        own_taps_ref[lag] = own_taps[:, :LANES]
        gate_taps_ref[lag : lag + 1, :] = taps_ref[lag, 0:1, :]
    rows = length // LANES
    chunk = min(1024, length)
    row_ids = lax.broadcasted_iota(jnp.int32, (feats, chunk), 0)
    band = jnp.where(row_ids > BANDS, row_ids - (BANDS + 1), row_ids - 1)
    band = jnp.clip(band, 0, BANDS - 1)
    quarter = jnp.where(row_ids <= BANDS, 0.25, 0.0)
    for start in range(0, length, chunk):
        places = lax.broadcasted_iota(jnp.int32, (feats, chunk), 1) + start
        phase = lax.shift_left(places, band) & (length - 1)
        turns = phase.astype(F32) * (1.0 / length)
        waves = sine_turns(turns + quarter)
        features = jnp.where(
            row_ids == 0,
            places.astype(F32) / length,
            jnp.where(row_ids <= 2 * BANDS, waves, 0.0),
        ).astype(BF16)
        first = sine(matmul(in_columns, features) + bias).astype(BF16)
        second = sine(matmul(mid_columns, first)).astype(BF16)
        ramp = (lax.broadcasted_iota(jnp.int32, (1, chunk), 1) + start).astype(F32) / length
        response = matmul(out_columns, second) * jnp.exp(-decay * ramp)
        for part in range(chunk // LANES):
            row = start // LANES + part
            response_ref[pl.ds(row, own, stride=rows), :] = response[:, part * LANES : (part + 1) * LANES]

    def one_group(step, carry):
        def load_pair(pair):
            base = (step * group + 2 * pair) * rows
            both = [
                response_ref[pl.ds(pl.multiple_of(base + side * rows, 8), rows), :] for side in range(2)
            ]
            high, low = split_parts(jnp.concatenate(both, 1))
            return jnp.concatenate([high, low, high], 0)

        spectrum = rows_to_spectrum(
            load_pair, group, forward_ref[...], turn_ref[0], turn_ref[1], square_ref[0], square_ref[1], padded
        )
        spectrum_ref[pl.ds(pl.multiple_of(step * group * padded, 8), group * padded), :] = spectrum
        return carry

    if own == group:
        one_group(0, 0)
    else:
        lax.fori_loop(0, own // group, one_group, 0)


def convolve_kernel(
    x_ref, taps_ref, direct_ref, gate_taps_ref, spectrum_hbm, turn_hbm, square_hbm, forward_hbm, inverse_hbm, out_hbm, side_ref,
    signal_ref, result_ref, out_ref, spectrum_ref, turn_ref, square_ref, forward_ref, inverse_ref,
    load_sems, out_sems, *, length, own, own_rows, group, tokens, places
):
    padded = turn_ref.shape[1]
    sources = (forward_hbm, turn_hbm, square_hbm, inverse_hbm, spectrum_hbm)
    targets = (forward_ref, turn_ref, square_ref, inverse_ref, spectrum_ref)
    loads = [pltpu.make_async_copy(s, t, load_sems.at[k]) for k, (s, t) in enumerate(zip(sources, targets))]
    for load in loads:
        load.start()
    rows = length // LANES
    per_block = tokens // LANES
    blocks = length // tokens
    seq_place = lax.axis_index("seq")
    width = side_ref.shape[1]
    count = width // LANES
    before = x_ref[jnp.maximum(seq_place - 1, 0), per_block * own_rows :, :].astype(F32)
    before = jnp.where(seq_place > 0, before, 0.0)
    side_ref[...] = jnp.zeros(side_ref.shape, F32)
    side_ref[:KSHORT, :] = gate_taps_ref[...]
    for k in range(2 * count):
        row, lanes = KSHORT + k // count, slice(k % count * LANES, (k % count + 1) * LANES)
        side_ref[row : row + 1, lanes] = before[8 + k : 9 + k, :]
    lane = lax.broadcasted_iota(jnp.int32, (own, LANES), 1)
    fixes = []
    last = [jnp.zeros((2, LANES), F32)] * 2
    for block in range(blocks):
        edge = x_ref[block, per_block * own_rows :, :].astype(F32)
        starts = []
        for role in range(2):
            here, before = edge[4 * role : 4 * role + 2], last[role]
            two_back = jnp.concatenate([before[1:2], here[0:1]], 0)
            starts.append(
                taps_ref[0, role + 1 : role + 2, :] * here
                + taps_ref[1, role + 1 : role + 2, :] * two_back
                + taps_ref[2, role + 1 : role + 2, :] * before
            )
            last[role] = edge[4 * role + 2 : 4 * role + 4]
        fixes.append(starts[1] * starts[0])
    fixed = jnp.concatenate(fixes, 0)
    if 2 * blocks < LANES:
        fixed = jnp.concatenate([fixed, jnp.zeros((LANES - 2 * blocks, LANES), F32)], 0)
    fixed = fixed.T[:own]
    for row in range(rows):
        block, part = divmod(row, per_block)
        values = x_ref[block, part * own_rows : part * own_rows + own, :].astype(F32)
        if part == 0:
            values = jnp.where(lane == 0, fixed[:, 2 * block : 2 * block + 1], values)
            values = jnp.where(lane == 1, fixed[:, 2 * block + 1 : 2 * block + 2], values)
        signal_ref[pl.ds(row, own, stride=rows), :] = values
    for load in loads[:3]:
        load.wait()
    turn_cos, turn_sin = turn_ref[0], turn_ref[1]

    def one_group(step, carry):
        def load_pair(pair):
            base = (step * group + 2 * pair) * rows
            both = [
                signal_ref[pl.ds(pl.multiple_of(base + side * rows, 8), rows), :] for side in range(2)
            ]
            values = jnp.concatenate(both, 1).astype(BF16)
            return jnp.concatenate([values, values], 0)

        signal = rows_to_spectrum(
            load_pair, group, forward_ref[...], turn_cos, turn_sin, square_ref[0], square_ref[1], padded
        )
        if own == group:
            for load in loads[3:]:
                load.wait()
        other = spectrum_ref[pl.ds(pl.multiple_of(step * group * padded, 8), group * padded), :]
        s_real, s_imag = signal[:, :LANES], signal[:, LANES:]
        f_real, f_imag = other[:, :LANES], other[:, LANES:]
        product = jnp.concatenate(
            [s_real * f_real - s_imag * f_imag, s_real * f_imag + s_imag * f_real], 1
        )
        high, low = split_parts(product)
        mixed = (
            matmul(high, square_ref[2]) + matmul(low, square_ref[2]) + matmul(high, square_ref[3])
        )
        for pair in range(group // 2):
            first = mixed[2 * pair * padded : (2 * pair + 1) * padded]
            second = mixed[(2 * pair + 1) * padded : (2 * pair + 2) * padded]
            real = jnp.concatenate([first[:, :LANES], second[:, :LANES]], 1)
            imag = jnp.concatenate([first[:, LANES:], second[:, LANES:]], 1)
            turned = jnp.concatenate(
                [real * turn_cos - imag * turn_sin, imag * turn_cos + real * turn_sin], 0
            )
            t_high, t_low = split_parts(turned)
            values = matmul(inverse_ref[...], jnp.concatenate([t_high, t_low, t_high], 0))
            base = (step * group + 2 * pair) * rows
            for side in range(2):
                result_ref[pl.ds(pl.multiple_of(base + side * rows, 8), rows), :] = values[
                    :, side * LANES : (side + 1) * LANES
                ]
        return carry

    if own == group:
        one_group(0, 0)
    else:
        for load in loads[3:]:
            load.wait()
        lax.fori_loop(0, own // group, one_group, 0)
    bias = direct_ref[...]
    share_rows = per_block // places
    blocks = length // tokens
    stores, half = [], max(blocks // 2, 1)
    for row in range(rows):
        block, part = divmod(row, per_block)
        place, side = divmod(part, share_rows)
        values = result_ref[pl.ds(row, own, stride=rows), :]
        values = values + bias * signal_ref[pl.ds(row, own, stride=rows), :]
        target = place * blocks + block
        out_ref[target, :, side * LANES : (side + 1) * LANES] = values.astype(BF16)
        if part == per_block - 1 and (block + 1) % half == 0:
            for p in range(places):
                span = pl.ds(p * blocks + block + 1 - half, half)
                store = pltpu.make_async_copy(out_ref.at[span], out_hbm.at[span], out_sems.at[len(stores)])
                store.start()
                stores.append(store)
    for store in stores:
        store.wait()


def gelu(values):
    return values * (lax.erf(values * np.float32(0.5**0.5)) + 1.0) * 0.5


def tail_kernel(
    z_ref, gate_ref, mix_ref, gain_ref, rows_hbm, *refs, pieces, share, width, block, rest
):
    mix_hbm, refs = refs[0], refs[1:]
    up_hbm, refs = refs[:pieces], refs[pieces:]
    down_hbm, refs = refs[:pieces], refs[pieces:]
    out_refs, refs = refs[:pieces], refs[pieces:]
    sums_ref, rows_ref, rest_ref, up_ref, down_ref, first_sems, up_sems, down_sems = refs
    total = pieces * width
    steps = up_ref.shape[2] // block
    count = pieces * steps
    firsts = [
        pltpu.make_async_copy(mix_hbm.at[pl.ds(width - rest, rest)], rest_ref, first_sems.at[0]),
        pltpu.make_async_copy(rows_hbm, rows_ref, first_sems.at[1]),
    ]
    ups, downs = [], []
    for p in range(pieces):
        for k in range(steps):
            cols = pl.ds(k * block, block)
            ups.append(pltpu.make_async_copy(up_hbm[p].at[:, cols], up_ref.at[p, :, cols], up_sems.at[p, k]))
            downs.append(pltpu.make_async_copy(down_hbm[p].at[cols], down_ref.at[p, cols], down_sems.at[p, k]))
    copies = list(firsts)
    for k in range(count + 2):
        copies += ups[k : k + 1]
        if k >= 2:
            copies.append(downs[k - 2])
    started, waited = [0], [0]

    def start_until(limit):
        while started[0] < min(limit, len(copies)):
            copies[started[0]].start()
            started[0] += 1

    def next_copy():
        start_until(waited[0] + AHEAD)
        copies[waited[0]].wait()
        waited[0] += 1

    start_until(AHEAD)
    me = lax.axis_index("chan")
    places = [lax.rem(me + p, pieces) for p in range(pieces)]
    dims = (((0,), (0,)), ((), ()))
    sums = 0.0
    for p in range(pieces):
        mixed = (z_ref[places[p]].astype(F32) * gate_ref[p]).astype(BF16)
        size = width - rest if p == pieces - 1 else width
        kept = mix_ref[p * width : p * width + size, :]
        sums = sums + lax.dot_general(mixed[:size], kept, dims, preferred_element_type=F32)
    next_copy()
    sums = sums + lax.dot_general(mixed[width - rest :], rest_ref[...], dims, preferred_element_type=F32)
    sums_ref[...] = sums
    next_copy()
    for p in range(pieces):
        cols = pl.ds(pl.multiple_of(places[p] * width, LANES), width)
        residual = rows_ref[p].astype(F32) + sums_ref[:, cols]
        sums_ref[:, cols] = residual.astype(BF16).astype(F32)
    values = sums_ref[...]
    mean = jnp.sum(values, axis=1, keepdims=True) / total
    centered = values - mean
    spread = jnp.sum(centered * centered, axis=1, keepdims=True) / total
    normed = (centered * lax.rsqrt(spread + EPS) * gain_ref[...]).astype(BF16)
    lifted = hidden = None
    for k in range(count + 2):
        new_lifted = new_hidden = None
        if k < count:
            next_copy()
            p, part = divmod(k, steps)
            new_lifted = matmul(normed, up_ref[p, :, part * block : (part + 1) * block])
        if lifted is not None:
            new_hidden = gelu(lifted).astype(BF16)
        if k >= 2:
            next_copy()
            p, part = divmod(k - 2, steps)
            sums_ref[...] += matmul(hidden, down_ref[p, part * block : (part + 1) * block, :])
        lifted, hidden = new_lifted, new_hidden
    for p in range(pieces):
        cols = pl.ds(pl.multiple_of(places[p] * width, LANES), width)
        out_refs[p][...] = sums_ref[:, cols].astype(BF16)


def join_kernel(*refs, pieces, share):
    out_hbm, sems = refs[pieces:]
    me = lax.axis_index("chan")
    copies = []
    for p in range(pieces):
        start = lax.rem(me + pieces - p, pieces) * share
        rows = pl.ds(pl.multiple_of(start, 16), share)
        copies.append(pltpu.make_async_copy(refs[p], out_hbm.at[rows], sems.at[p]))
    for copy in copies:
        copy.start()
    for copy in copies:
        copy.wait()


HBM = pl.BlockSpec(memory_space=pltpu.HBM)
VMEM = pl.BlockSpec(memory_space=pltpu.VMEM)


def call(kernel, in_specs, out_specs, out_shape, scratch, megabytes, *args):
    kinds = {"h": HBM, "v": VMEM, "c": VMEM}
    spaces = {"h": pltpu.HBM, "v": pltpu.VMEM, "c": pltpu.HBM}
    placed = [
        pltpu.with_memory_space_constraint(arg, spaces[kind])
        for kind, arg in zip(in_specs, args, strict=True)
    ]
    return pl.pallas_call(
        kernel,
        in_specs=[kinds[kind] for kind in in_specs],
        out_specs=out_specs,
        out_shape=out_shape,
        scratch_shapes=scratch,
        compiler_params=pltpu.CompilerParams(vmem_limit_bytes=megabytes * 1024 * 1024),
    )(*placed)


def shape_of(shape, dtype):
    return jax.ShapeDtypeStruct(shape, dtype)


def per_device(
    layer_input, gain_first, in_weight, short_weight, filt_in, filt_bias, filt_mid, filt_out,
    decay_rate, conv_bias, out_weight, gain_second, up_weight, down_weight,
):
    tokens, width = layer_input.shape
    pieces = lax.axis_size("chan")
    groups = lax.axis_size("seq")
    model = pieces * width
    length = tokens * groups
    share = tokens // pieces
    own = width // groups
    own_rows = -(-own // 16) * 16
    block_rows = tokens // LANES * own_rows + 16

    def turned(array, by):
        if by == 0:
            return array
        return lax.ppermute(array, "chan", [(i, (i - by) % pieces) for i in range(pieces)])

    def all_turned(array):
        return [turned(array, p) for p in range(pieces)]

    x_pieces = all_turned(layer_input)
    by_role = jnp.transpose(in_weight, (1, 0, 2))
    step = min(width, 256)
    normed, my_rows, gated = call(
        functools.partial(
            project_kernel, pieces=pieces, tokens=tokens, width=width, own=own, own_rows=own_rows, share=share
        ),
        "c" + "v" * (pieces - 1) + "cch",
        (HBM, HBM, HBM),
        (
            pltpu.HBM((pieces, tokens, width), BF16),
            pltpu.HBM((pieces, share, width), BF16),
            pltpu.HBM((groups, block_rows, LANES), BF16),
        ),
        [
            pltpu.VMEM((3, model, width), BF16),
            pltpu.VMEM((2, tokens + 8, step), F32),
            pltpu.VMEM((groups, block_rows, LANES), BF16),
            pltpu.VMEM((pieces, tokens, width), BF16),
            pltpu.SemaphoreType.DMA((3,)),
            pltpu.SemaphoreType.DMA((width // step,)),
            pltpu.SemaphoreType.DMA,
            pltpu.SemaphoreType.DMA((pieces,)),
        ],
        20,
        *x_pieces, gain_first.reshape(pieces, 1, width), short_weight, by_role,
    )
    by_role, out_weight, up_weight, down_weight, gated = lax.optimization_barrier(
        (by_role, out_weight, up_weight, down_weight, gated)
    )
    regrouped = lax.all_to_all(gated, "seq", split_axis=0, concat_axis=0, tiled=True)

    tables = {name: jnp.asarray(table) for name, table in transform_tables(length).items()}
    padded = tables["turn"].shape[1]
    rows = length // LANES
    filters = filt_mid.shape[0]
    spectrum, own_taps, own_direct, gate_taps = call(
        functools.partial(filter_kernel, length=length, own=own, group=own),
        "c" * 10,
        (VMEM,) * 4,
        (
            pltpu.HBM((own * padded, 2 * LANES), F32),
            pltpu.VMEM((KSHORT, 8, LANES), F32),
            pltpu.VMEM((own, LANES), F32),
            pltpu.VMEM((KSHORT, width), F32),
        ),
        [
            pltpu.VMEM((own * rows, LANES), F32),
            pltpu.VMEM((width, filters), F32),
            pltpu.VMEM((width, 8), F32),
            pltpu.VMEM((32, filters), F32),
        ],
        24,
        filt_in, filt_bias[None, :], filt_mid, filt_out, decay_rate[None, :], conv_bias[None, :],
        short_weight, tables["turn"], tables["square"], tables["forward3"],
    )
    places = pieces if share % LANES == 0 else 1
    kept_tables = [tables[name] for name in ("turn", "square", "forward2", "inverse3")]
    convolved, side = call(
        functools.partial(
            convolve_kernel, length=length, own=own, own_rows=own_rows, group=own, tokens=tokens, places=places
        ),
        "vvvv" + "h" * 5,
        (HBM, VMEM),
        (pltpu.HBM((places * groups, own, tokens // places), BF16), shape_of((8, width), F32)),
        [
            pltpu.VMEM((own * rows, LANES), F32),
            pltpu.VMEM((own * rows, LANES), F32),
            pltpu.VMEM((places * groups, own, tokens // places), BF16),
            *(pltpu.VMEM(array.shape, array.dtype) for array in (spectrum, *kept_tables)),
            pltpu.SemaphoreType.DMA((5,)),
            pltpu.SemaphoreType.DMA((2 * places,)),
        ],
        40,
        regrouped, own_taps, own_direct, gate_taps, spectrum, *kept_tables,
    )
    if places != pieces:
        convolved = jnp.transpose(convolved.reshape(groups, own, pieces, share), (2, 0, 1, 3))
        convolved = convolved.reshape(pieces * groups, own, share)
    returned = lax.all_to_all(convolved, ("chan", "seq"), split_axis=0, concat_axis=0, tiled=True)
    returned = returned.reshape(pieces, width, share)

    mix_weights = all_turned(out_weight)
    up_weights = all_turned(up_weight)
    down_weights = all_turned(down_weight)
    rest = 64
    gate, mix_kept = call(
        functools.partial(gate_kernel, pieces=pieces, share=share, width=width, rest=rest),
        "c" + "v" * pieces + "h" * (2 * pieces),
        (VMEM, VMEM),
        (pltpu.VMEM((pieces, width, share), F32), pltpu.VMEM((model - rest, model), BF16)),
        [
            pltpu.VMEM((pieces, model, width), BF16),
            pltpu.VMEM((pieces, share + HALO, width), BF16),
            pltpu.VMEM((share + HALO, width), F32),
            pltpu.SemaphoreType.DMA((pieces,)),
            pltpu.SemaphoreType.DMA((pieces,)),
        ],
        16,
        normed, *all_turned(side), *all_turned(by_role), *mix_weights,
    )
    units = up_weight.shape[1]
    block = min(512, units)
    results = call(
        functools.partial(tail_kernel, pieces=pieces, share=share, width=width, block=block, rest=rest),
        "vvvch" + "h" * (1 + 2 * pieces),
        (VMEM,) * pieces,
        tuple(shape_of((share, width), BF16) for p in range(pieces)),
        [
            pltpu.VMEM((share, model), F32),
            pltpu.VMEM((pieces, share, width), BF16),
            pltpu.VMEM((rest, model), BF16),
            pltpu.VMEM((pieces, model, units), BF16),
            pltpu.VMEM((pieces, units, model), BF16),
            pltpu.SemaphoreType.DMA((2,)),
            pltpu.SemaphoreType.DMA((pieces, units // block)),
            pltpu.SemaphoreType.DMA((pieces, units // block)),
        ],
        44,
        returned, gate, mix_kept, gain_second[None, :], my_rows, mix_weights[-1], *up_weights, *down_weights,
    )
    received = [results[0]] + [
        lax.ppermute(results[p], "chan", [(i, (i + p) % pieces) for i in range(pieces)])
        for p in range(1, pieces)
    ]
    return call(
        functools.partial(join_kernel, pieces=pieces, share=share),
        "v" * pieces,
        HBM,
        pltpu.HBM((tokens, width), BF16),
        [pltpu.SemaphoreType.DMA((pieces,))],
        8,
        *received,
    )


def solution(mesh):
    placed = (
        P("seq", "chan"),
        P(),
        P(None, None, "chan"),
        P(None, None, "chan"),
        P(),
        P(),
        P(),
        P(None, "chan"),
        P("chan"),
        P("chan"),
        P("chan", None),
        P(),
        P(None, "chan"),
        P("chan", None),
    )
    return jax.shard_map(
        per_device, mesh=mesh, in_specs=placed, out_specs=P("seq", "chan"), check_vma=False
    )
```

```python
import functools

import jax
import jax.numpy as jnp
import ml_dtypes
import numpy as np
from jax import lax
from jax.experimental import pallas as pl
from jax.experimental.pallas import tpu as pltpu
from jax.sharding import PartitionSpec as P

BANDS = 12
KSHORT = 3
LANES = 128
HALO = 16
AHEAD = 6
EPS = 1e-05
PI_HIGH = 3.140625
PI_LOW = 9.67653589793e-4
F32 = jnp.float32
BF16 = jnp.bfloat16
VMEM_BYTES = 60 * 1024 * 1024


def matmul(left, right):
    return jnp.dot(left, right, preferred_element_type=F32)


def split_parts(values):
    high = values.astype(BF16)
    return high, (values - high.astype(F32)).astype(BF16)


def split_table(table):
    high = table.astype(np.float32).astype(ml_dtypes.bfloat16)
    low = (table - high.astype(np.float64)).astype(np.float32).astype(ml_dtypes.bfloat16)
    return high, low


def transform_tables(length):
    rows = length // LANES
    period = 2 * rows
    full = 2 * length
    kept = rows + 1
    padded = -(-kept // 8) * 8
    k2 = np.arange(padded)
    valid = (k2 < kept).astype(np.float64)[:, None]
    n2 = np.arange(rows)
    n1 = np.arange(LANES)
    first = 2 * np.pi / period * (k2[:, None] * n2[None, :] % period)
    forward = np.concatenate([np.cos(first) * valid, -np.sin(first) * valid], 0)
    weight = np.where((k2 == 0) | (k2 == rows), 1.0, 2.0)[:, None] * valid
    inverse = np.concatenate([np.cos(first) * weight, -np.sin(first) * weight], 0).T
    turn = 2 * np.pi / full * (k2[:, None] * n1[None, :] % full)
    second = 2 * np.pi / LANES * (n1[:, None] * n1[None, :] % LANES)
    cos2, sin2 = np.cos(second), np.sin(second)
    mid = np.concatenate(
        [np.concatenate([cos2, -sin2], 1), np.concatenate([sin2, cos2], 1)], 0
    )
    back = np.concatenate(
        [np.concatenate([cos2, sin2], 1), np.concatenate([-sin2, cos2], 1)], 0
    ) / full
    f_high, f_low = split_table(forward)
    i_high, i_low = split_table(inverse)
    f_high, f_low = split_table(forward)
    i_high, i_low = split_table(inverse)
    return {
        "turn": np.tile(np.stack([np.cos(turn), np.sin(turn)]), (1, 1, 2)).astype(np.float32),
        "square": np.stack([*split_table(mid), *split_table(back)]),
        "forward3": np.concatenate([f_high, f_high, f_low], 1),
        "forward2": np.concatenate([f_high, f_low], 1),
        "inverse3": np.concatenate([i_high, i_high, i_low], 1),
    }


def sine(values):
    count = jnp.floor(values * (1.0 / np.pi) + 0.5)
    rest = (values - count * PI_HIGH) - count * PI_LOW
    half = count * 0.5
    sign = 1.0 - 4.0 * (half - jnp.floor(half))
    return sign * sine_poly(rest)


def sine_poly(rest):
    square = rest * rest
    poly = -2.5052108385441720e-08
    poly = poly * square + 2.7557319223985893e-06
    poly = poly * square - 1.9841269841269841e-04
    poly = poly * square + 8.3333333333333333e-03
    poly = poly * square - 1.6666666666666667e-01
    return rest + rest * square * poly


def sine_turns(turns):
    count = jnp.floor(turns * 2.0 + 0.5)
    rest = (turns - count * 0.5) * (2.0 * np.pi)
    half = count * 0.5
    sign = 1.0 - 4.0 * (half - jnp.floor(half))
    return sign * sine_poly(rest)


def rows_to_spectrum(load_pair, group, table, turn_cos, turn_sin, mid_high, mid_low, padded):
    stacked = []
    for pair in range(group // 2):
        first = matmul(table, load_pair(pair))
        real, imag = first[:padded], first[padded:]
        turned_real = real * turn_cos + imag * turn_sin
        turned_imag = imag * turn_cos - real * turn_sin
        for side in range(2):
            lanes = slice(side * LANES, (side + 1) * LANES)
            stacked.append(jnp.concatenate([turned_real[:, lanes], turned_imag[:, lanes]], 1))
    if mid_low is None:
        return matmul(jnp.concatenate(stacked, 0).astype(BF16), mid_high)
    high, low = split_parts(jnp.concatenate(stacked, 0))
    return matmul(high, mid_high) + matmul(low, mid_high) + matmul(high, mid_low)


def project_kernel(
    *refs, pieces, tokens, width, own, own_rows, share
):
    x_refs, refs = refs[:pieces], refs[pieces:]
    gain_ref, taps_ref, w_hbm, normed_hbm, rows_hbm, out_hbm, refs = *refs[:6], refs[6:]
    w_ref, proj_ref, block_ref, normed_ref, w_sems, out_sems, normed_sem, row_sems = refs
    me = lax.axis_index("chan")
    places = [lax.rem(me + p, pieces) for p in range(pieces)]
    total = pieces * width
    loads = [pltpu.make_async_copy(w_hbm.at[(role + 1) % 3], w_ref.at[role], w_sems.at[role]) for role in range(3)]
    for load in loads:
        load.start()
    chunk = 128
    for start in range(0, tokens, chunk):
        values = [ref[start : start + chunk, :].astype(F32) for ref in x_refs]
        mean = sum(jnp.sum(v, axis=1, keepdims=True) for v in values) / total
        centered = [v - mean for v in values]
        spread = sum(jnp.sum(c * c, axis=1, keepdims=True) for c in centered) / total
        scale = lax.rsqrt(spread + EPS)
        for p in range(pieces):
            gain = gain_ref[places[p]]
            normed_ref[p, start : start + chunk, :] = (centered[p] * scale * gain).astype(BF16)
    mine = pl.ds(pl.multiple_of(me * share, 16), share)
    keeps = [pltpu.make_async_copy(normed_ref, normed_hbm, normed_sem)]
    for p in range(pieces):
        keeps.append(pltpu.make_async_copy(x_refs[p].at[mine], rows_hbm.at[p], row_sems.at[p]))
    for keep in keeps:
        keep.start()
    step = min(width, 256)
    per_step = step // own
    parts = tokens // LANES
    proj_ref[:, :8, :] = jnp.zeros((2, 8, step), F32)
    for load in loads[:2]:
        load.wait()
    stores = []
    for col in range(0, width, step):
        cols = slice(col, col + step)
        for role in range(2):
            sums = 0.0
            for p in range(pieces):
                rows = pl.ds(pl.multiple_of(places[p] * width, width), width)
                sums = sums + matmul(normed_ref[p], w_ref[role, rows, cols])
            proj_ref[role, 8:, :] = sums.astype(BF16).astype(F32)
        shorted = []
        for role in range(2):
            value = taps_ref[0, role + 1 : role + 2, cols] * proj_ref[role, 8 : 8 + tokens, :]
            for lag in range(1, KSHORT):
                value = (
                    value
                    + taps_ref[lag, role + 1 : role + 2, cols] * proj_ref[role, 8 - lag : 8 - lag + tokens, :]
                )
            shorted.append(value)
        gated = (shorted[1] * shorted[0]).T
        if col == 0:
            loads[2].wait()
            last = 0.0
            for p in range(pieces):
                rows = pl.ds(pl.multiple_of(places[p] * width, width), width)
                last = last + matmul(normed_ref[p, tokens - HALO :, :], w_ref[2, rows, :])
            last = last.astype(BF16).astype(F32)
            spread_last = [
                last[row : row + 1, lane : lane + LANES]
                for row in (HALO - 2, HALO - 1)
                for lane in range(0, width, LANES)
            ]
            spread_last = jnp.concatenate(spread_last + [jnp.zeros((8 - len(spread_last), LANES), F32)][: len(spread_last) < 8], 0)
        edges = jnp.concatenate(
            [
                proj_ref[0, 8:10, :],
                proj_ref[0, 6 + tokens : 8 + tokens, :],
                proj_ref[1, 8:10, :],
                proj_ref[1, 6 + tokens : 8 + tokens, :],
            ],
            0,
        )
        first = col // own
        for d in range(per_step):
            for part in range(parts):
                block_ref[first + d, part * own_rows : part * own_rows + own, :] = gated[
                    d * own : (d + 1) * own, part * LANES : (part + 1) * LANES
                ].astype(BF16)
            block_edges = jnp.concatenate([edges[:, d * own : (d + 1) * own], jnp.zeros((8, LANES - own), F32)], 1)
            block_ref[first + d, parts * own_rows :, :] = jnp.concatenate([block_edges, spread_last], 0).astype(BF16)
        targets = pl.ds(first, per_step)
        store = pltpu.make_async_copy(block_ref.at[targets], out_hbm.at[targets], out_sems.at[col // step])
        store.start()
        stores.append(store)
    for store in stores:
        store.wait()
    for keep in keeps:
        keep.wait()


def gate_kernel(normed_ref, *refs, pieces, share, width, rest):
    side_refs, refs = refs[:pieces], refs[pieces:]
    w_hbm, refs = refs[:pieces], refs[pieces:]
    mix_hbm, (gate_ref, mix_ref, w_ref, rows_ref, proj_ref, w_sems, mix_sems) = refs[:pieces], refs[pieces:]
    fetches = []
    for p in range(pieces):
        size = width - rest if p == pieces - 1 else width
        fetches.append(
            pltpu.make_async_copy(
                mix_hbm[p].at[pl.ds(0, size)], mix_ref.at[pl.ds(p * width, size)], mix_sems.at[p]
            )
        )
    loads = [pltpu.make_async_copy(w_hbm[p].at[0], w_ref.at[p], w_sems.at[p]) for p in range(pieces)]
    for load in loads + fetches:
        load.start()
    me = lax.axis_index("chan")
    places = [lax.rem(me + p, pieces) for p in range(pieces)]
    mine = pl.ds(pl.multiple_of(me * share, 16), share)
    before = pl.ds(pl.multiple_of(jnp.maximum(me * share - HALO, 0), 16), HALO)
    for p in range(pieces):
        rows_ref[p, HALO:, :] = normed_ref[p, mine, :]
        rows_ref[p, :HALO, :] = normed_ref[p, before, :]
    for load in loads:
        load.wait()
    for out in range(pieces):
        sums = 0.0
        for p in range(pieces):
            rows = pl.ds(pl.multiple_of(places[p] * width, width), width)
            sums = sums + matmul(rows_ref[p], w_ref[out, rows, :])
        proj_ref[...] = sums.astype(BF16).astype(F32)
        proj_ref[HALO - 2 : HALO, :] = jnp.where(
            me == 0, side_refs[out][KSHORT : KSHORT + 2, :], proj_ref[HALO - 2 : HALO, :]
        )
        value = side_refs[out][0:1, :] * proj_ref[HALO : HALO + share, :]
        for lag in range(1, KSHORT):
            value = value + side_refs[out][lag : lag + 1, :] * proj_ref[HALO - lag : HALO - lag + share, :]
        gate_ref[out] = value.T
    for fetch in fetches:
        fetch.wait()


def filter_kernel(
    in_ref, bias_ref, mid_w_ref, out_w_ref, decay_ref, direct_ref, taps_ref,
    turn_ref, square_ref, forward_ref, spectrum_ref, own_taps_ref, own_direct_ref, gate_taps_ref,
    response_ref, columns_ref, scalars_ref, in_pad_ref, *, length, own, group
):
    padded = turn_ref.shape[1]
    seq_place = lax.axis_index("seq")
    width = out_w_ref.shape[1]
    feats = in_pad_ref.shape[0]
    in_pad_ref[...] = jnp.zeros(in_pad_ref.shape, F32)
    in_pad_ref[: in_ref.shape[0], :] = in_ref[...].astype(F32)
    in_columns = in_pad_ref[...].T.astype(BF16)
    mid_columns = mid_w_ref[...].astype(F32).T.astype(BF16)
    bias = jnp.broadcast_to(bias_ref[...], (8, bias_ref.shape[1])).T[:, :1]
    columns_ref[...] = out_w_ref[...].astype(F32).T
    scalars_ref[...] = jnp.concatenate(
        [jnp.broadcast_to(decay_ref[...], (4, width)), jnp.broadcast_to(direct_ref[...], (4, width))], 0
    ).T
    mine = pl.ds(seq_place * own, own)
    out_columns = columns_ref[mine, :].astype(BF16)
    decay = scalars_ref[mine, 0:1]
    own_direct_ref[...] = jnp.broadcast_to(scalars_ref[mine, 4:5], (own, LANES))
    shift = lax.rem(width - seq_place * own, width)
    for lag in range(KSHORT):
        own_taps = pltpu.roll(jnp.concatenate([taps_ref[lag], jnp.zeros((5, width), F32)], 0), shift, 1)
        own_taps_ref[lag] = own_taps[:, :LANES]
        gate_taps_ref[lag : lag + 1, :] = taps_ref[lag, 0:1, :]
    rows = length // LANES
    chunk = min(1024, length)
    row_ids = lax.broadcasted_iota(jnp.int32, (feats, chunk), 0)
    band = jnp.where(row_ids > BANDS, row_ids - (BANDS + 1), row_ids - 1)
    band = jnp.clip(band, 0, BANDS - 1)
    quarter = jnp.where(row_ids <= BANDS, 0.25, 0.0)
    for start in range(0, length, chunk):
        places = lax.broadcasted_iota(jnp.int32, (feats, chunk), 1) + start
        phase = lax.shift_left(places, band) & (length - 1)
        turns = phase.astype(F32) * (1.0 / length)
        waves = sine_turns(turns + quarter)
        features = jnp.where(
            row_ids == 0,
            places.astype(F32) / length,
            jnp.where(row_ids <= 2 * BANDS, waves, 0.0),
        ).astype(BF16)
        first = sine(matmul(in_columns, features) + bias).astype(BF16)
        second = sine(matmul(mid_columns, first)).astype(BF16)
        ramp = (lax.broadcasted_iota(jnp.int32, (1, chunk), 1) + start).astype(F32) / length
        response = matmul(out_columns, second) * jnp.exp(-decay * ramp)
        for part in range(chunk // LANES):
            row = start // LANES + part
            response_ref[pl.ds(row, own, stride=rows), :] = response[:, part * LANES : (part + 1) * LANES]

    def one_group(step, carry):
        def load_pair(pair):
            base = (step * group + 2 * pair) * rows
            both = [
                response_ref[pl.ds(pl.multiple_of(base + side * rows, 8), rows), :] for side in range(2)
            ]
            high, low = split_parts(jnp.concatenate(both, 1))
            return jnp.concatenate([high, low, high], 0)

        spectrum = rows_to_spectrum(
            load_pair, group, forward_ref[...], turn_ref[0], turn_ref[1], square_ref[0], square_ref[1], padded
        )
        spectrum_ref[pl.ds(pl.multiple_of(step * group * padded, 8), group * padded), :] = spectrum
        return carry

    if own == group:
        one_group(0, 0)
    else:
        lax.fori_loop(0, own // group, one_group, 0)


def convolve_kernel(
    x_ref, taps_ref, direct_ref, gate_taps_ref, spectrum_hbm, turn_hbm, square_hbm, forward_hbm, inverse_hbm, out_hbm, side_ref,
    signal_ref, result_ref, out_ref, spectrum_ref, turn_ref, square_ref, forward_ref, inverse_ref,
    load_sems, out_sems, *, length, own, own_rows, group, tokens, places
):
    padded = turn_ref.shape[1]
    sources = (forward_hbm, turn_hbm, square_hbm, inverse_hbm, spectrum_hbm)
    targets = (forward_ref, turn_ref, square_ref, inverse_ref, spectrum_ref)
    loads = [pltpu.make_async_copy(s, t, load_sems.at[k]) for k, (s, t) in enumerate(zip(sources, targets))]
    for load in loads:
        load.start()
    rows = length // LANES
    per_block = tokens // LANES
    blocks = length // tokens
    seq_place = lax.axis_index("seq")
    width = side_ref.shape[1]
    count = width // LANES
    before = x_ref[jnp.maximum(seq_place - 1, 0), per_block * own_rows :, :].astype(F32)
    before = jnp.where(seq_place > 0, before, 0.0)
    side_ref[...] = jnp.zeros(side_ref.shape, F32)
    side_ref[:KSHORT, :] = gate_taps_ref[...]
    for k in range(2 * count):
        row, lanes = KSHORT + k // count, slice(k % count * LANES, (k % count + 1) * LANES)
        side_ref[row : row + 1, lanes] = before[8 + k : 9 + k, :]
    lane = lax.broadcasted_iota(jnp.int32, (own, LANES), 1)
    fixes = []
    last = [jnp.zeros((2, LANES), F32)] * 2
    for block in range(blocks):
        edge = x_ref[block, per_block * own_rows :, :].astype(F32)
        starts = []
        for role in range(2):
            here, before = edge[4 * role : 4 * role + 2], last[role]
            two_back = jnp.concatenate([before[1:2], here[0:1]], 0)
            starts.append(
                taps_ref[0, role + 1 : role + 2, :] * here
                + taps_ref[1, role + 1 : role + 2, :] * two_back
                + taps_ref[2, role + 1 : role + 2, :] * before
            )
            last[role] = edge[4 * role + 2 : 4 * role + 4]
        fixes.append(starts[1] * starts[0])
    fixed = jnp.concatenate(fixes, 0)
    if 2 * blocks < LANES:
        fixed = jnp.concatenate([fixed, jnp.zeros((LANES - 2 * blocks, LANES), F32)], 0)
    fixed = fixed.T[:own]
    for row in range(rows):
        block, part = divmod(row, per_block)
        values = x_ref[block, part * own_rows : part * own_rows + own, :].astype(F32)
        if part == 0:
            values = jnp.where(lane == 0, fixed[:, 2 * block : 2 * block + 1], values)
            values = jnp.where(lane == 1, fixed[:, 2 * block + 1 : 2 * block + 2], values)
        signal_ref[pl.ds(row, own, stride=rows), :] = values
    for load in loads[:3]:
        load.wait()
    turn_cos, turn_sin = turn_ref[0], turn_ref[1]

    def one_group(step, carry):
        def load_pair(pair):
            base = (step * group + 2 * pair) * rows
            both = [
                signal_ref[pl.ds(pl.multiple_of(base + side * rows, 8), rows), :] for side in range(2)
            ]
            values = jnp.concatenate(both, 1).astype(BF16)
            return jnp.concatenate([values, values], 0)

        signal = rows_to_spectrum(
            load_pair, group, forward_ref[...], turn_cos, turn_sin, square_ref[0], None, padded
        )
        if own == group:
            for load in loads[3:]:
                load.wait()
        other = spectrum_ref[pl.ds(pl.multiple_of(step * group * padded, 8), group * padded), :]
        s_real, s_imag = signal[:, :LANES], signal[:, LANES:]
        f_real, f_imag = other[:, :LANES], other[:, LANES:]
        product = jnp.concatenate(
            [s_real * f_real - s_imag * f_imag, s_real * f_imag + s_imag * f_real], 1
        )
        mixed = matmul(product.astype(BF16), square_ref[2])
        for pair in range(group // 2):
            first = mixed[2 * pair * padded : (2 * pair + 1) * padded]
            second = mixed[(2 * pair + 1) * padded : (2 * pair + 2) * padded]
            real = jnp.concatenate([first[:, :LANES], second[:, :LANES]], 1)
            imag = jnp.concatenate([first[:, LANES:], second[:, LANES:]], 1)
            turned = jnp.concatenate(
                [real * turn_cos - imag * turn_sin, imag * turn_cos + real * turn_sin], 0
            )
            t_high, t_low = split_parts(turned)
            values = matmul(inverse_ref[...], jnp.concatenate([t_high, t_low, t_high], 0))
            base = (step * group + 2 * pair) * rows
            for side in range(2):
                result_ref[pl.ds(pl.multiple_of(base + side * rows, 8), rows), :] = values[
                    :, side * LANES : (side + 1) * LANES
                ]
        return carry

    if own == group:
        one_group(0, 0)
    else:
        for load in loads[3:]:
            load.wait()
        lax.fori_loop(0, own // group, one_group, 0)
    bias = direct_ref[...]
    share_rows = per_block // places
    blocks = length // tokens
    stores, half = [], max(blocks // 2, 1)
    for row in range(rows):
        block, part = divmod(row, per_block)
        place, side = divmod(part, share_rows)
        values = result_ref[pl.ds(row, own, stride=rows), :]
        values = values + bias * signal_ref[pl.ds(row, own, stride=rows), :]
        target = block * places + place
        out_ref[target, :, side * LANES : (side + 1) * LANES] = values.astype(BF16)
        if part == per_block - 1 and (block + 1) % half == 0:
            span = pl.ds((block + 1 - half) * places, half * places)
            store = pltpu.make_async_copy(out_ref.at[span], out_hbm.at[span], out_sems.at[len(stores)])
            store.start()
            stores.append(store)
    for store in stores:
        store.wait()


def gelu(values):
    return values * (lax.erf(values * np.float32(0.5**0.5)) + 1.0) * 0.5


def tail_kernel(
    z_ref, gate_ref, mix_ref, gain_ref, rows_hbm, *refs, pieces, share, width, block, rest
):
    mix_hbm, refs = refs[0], refs[1:]
    up_hbm, refs = refs[:pieces], refs[pieces:]
    down_hbm, refs = refs[:pieces], refs[pieces:]
    out_refs, refs = refs[:pieces], refs[pieces:]
    sums_ref, rows_ref, rest_ref, up_ref, down_ref, first_sems, up_sems, down_sems = refs
    total = pieces * width
    steps = up_ref.shape[2] // block
    count = pieces * steps
    firsts = [
        pltpu.make_async_copy(mix_hbm.at[pl.ds(width - rest, rest)], rest_ref, first_sems.at[0]),
        pltpu.make_async_copy(rows_hbm, rows_ref, first_sems.at[1]),
    ]
    ups, downs = [], []
    for p in range(pieces):
        for k in range(steps):
            cols = pl.ds(k * block, block)
            ups.append(pltpu.make_async_copy(up_hbm[p].at[:, cols], up_ref.at[p, :, cols], up_sems.at[p, k]))
            downs.append(pltpu.make_async_copy(down_hbm[p].at[cols], down_ref.at[p, cols], down_sems.at[p, k]))
    copies = list(firsts)
    for k in range(count + 2):
        copies += ups[k : k + 1]
        if k >= 2:
            copies.append(downs[k - 2])
    started, waited = [0], [0]

    def start_until(limit):
        while started[0] < min(limit, len(copies)):
            copies[started[0]].start()
            started[0] += 1

    def next_copy():
        start_until(waited[0] + AHEAD)
        copies[waited[0]].wait()
        waited[0] += 1

    start_until(AHEAD)
    me = lax.axis_index("chan")
    places = [lax.rem(me + p, pieces) for p in range(pieces)]
    dims = (((0,), (0,)), ((), ()))
    sums = 0.0
    for p in range(pieces):
        mixed = (z_ref[:, places[p]].reshape(width, share).astype(F32) * gate_ref[p]).astype(BF16)
        size = width - rest if p == pieces - 1 else width
        kept = mix_ref[p * width : p * width + size, :]
        sums = sums + lax.dot_general(mixed[:size], kept, dims, preferred_element_type=F32)
    next_copy()
    sums = sums + lax.dot_general(mixed[width - rest :], rest_ref[...], dims, preferred_element_type=F32)
    sums_ref[...] = sums
    next_copy()
    for p in range(pieces):
        cols = pl.ds(pl.multiple_of(places[p] * width, LANES), width)
        residual = rows_ref[p].astype(F32) + sums_ref[:, cols]
        sums_ref[:, cols] = residual.astype(BF16).astype(F32)
    values = sums_ref[...]
    mean = jnp.sum(values, axis=1, keepdims=True) / total
    centered = values - mean
    spread = jnp.sum(centered * centered, axis=1, keepdims=True) / total
    normed = (centered * lax.rsqrt(spread + EPS) * gain_ref[...]).astype(BF16)
    lifted = hidden = None
    for k in range(count + 2):
        new_lifted = new_hidden = None
        if k < count:
            next_copy()
            p, part = divmod(k, steps)
            new_lifted = matmul(normed, up_ref[p, :, part * block : (part + 1) * block])
        if lifted is not None:
            new_hidden = gelu(lifted).astype(BF16)
        if k >= 2:
            next_copy()
            p, part = divmod(k - 2, steps)
            sums_ref[...] += matmul(hidden, down_ref[p, part * block : (part + 1) * block, :])
        lifted, hidden = new_lifted, new_hidden
    for p in range(pieces):
        cols = pl.ds(pl.multiple_of(places[p] * width, LANES), width)
        out_refs[p][...] = sums_ref[:, cols].astype(BF16)


def join_kernel(*refs, pieces, share):
    out_hbm, sems = refs[pieces:]
    me = lax.axis_index("chan")
    copies = []
    for p in range(pieces):
        start = lax.rem(me + pieces - p, pieces) * share
        rows = pl.ds(pl.multiple_of(start, 16), share)
        copies.append(pltpu.make_async_copy(refs[p], out_hbm.at[rows], sems.at[p]))
    for copy in copies:
        copy.start()
    for copy in copies:
        copy.wait()


HBM = pl.BlockSpec(memory_space=pltpu.HBM)
VMEM = pl.BlockSpec(memory_space=pltpu.VMEM)


def call(kernel, in_specs, out_specs, out_shape, scratch, megabytes, *args):
    kinds = {"h": HBM, "v": VMEM, "c": VMEM}
    spaces = {"h": pltpu.HBM, "v": pltpu.VMEM, "c": pltpu.HBM}
    placed = [
        pltpu.with_memory_space_constraint(arg, spaces[kind])
        for kind, arg in zip(in_specs, args, strict=True)
    ]
    return pl.pallas_call(
        kernel,
        in_specs=[kinds[kind] for kind in in_specs],
        out_specs=out_specs,
        out_shape=out_shape,
        scratch_shapes=scratch,
        compiler_params=pltpu.CompilerParams(vmem_limit_bytes=megabytes * 1024 * 1024),
    )(*placed)


def shape_of(shape, dtype):
    return jax.ShapeDtypeStruct(shape, dtype)


def per_device(
    layer_input, gain_first, in_weight, short_weight, filt_in, filt_bias, filt_mid, filt_out,
    decay_rate, conv_bias, out_weight, gain_second, up_weight, down_weight,
):
    tokens, width = layer_input.shape
    pieces = lax.axis_size("chan")
    groups = lax.axis_size("seq")
    model = pieces * width
    length = tokens * groups
    share = tokens // pieces
    own = width // groups
    own_rows = -(-own // 16) * 16
    block_rows = tokens // LANES * own_rows + 16

    def turned(array, by):
        if by == 0:
            return array
        return lax.ppermute(array, "chan", [(i, (i - by) % pieces) for i in range(pieces)])

    def all_turned(array):
        return [turned(array, p) for p in range(pieces)]

    x_pieces = all_turned(layer_input)
    by_role = jnp.transpose(in_weight, (1, 0, 2))
    step = min(width, 256)
    normed, my_rows, gated = call(
        functools.partial(
            project_kernel, pieces=pieces, tokens=tokens, width=width, own=own, own_rows=own_rows, share=share
        ),
        "c" + "v" * (pieces - 1) + "cch",
        (HBM, HBM, HBM),
        (
            pltpu.HBM((pieces, tokens, width), BF16),
            pltpu.HBM((pieces, share, width), BF16),
            pltpu.HBM((groups, block_rows, LANES), BF16),
        ),
        [
            pltpu.VMEM((3, model, width), BF16),
            pltpu.VMEM((2, tokens + 8, step), F32),
            pltpu.VMEM((groups, block_rows, LANES), BF16),
            pltpu.VMEM((pieces, tokens, width), BF16),
            pltpu.SemaphoreType.DMA((3,)),
            pltpu.SemaphoreType.DMA((width // step,)),
            pltpu.SemaphoreType.DMA,
            pltpu.SemaphoreType.DMA((pieces,)),
        ],
        20,
        *x_pieces, gain_first.reshape(pieces, 1, width), short_weight, by_role,
    )
    by_role, out_weight, up_weight, down_weight, gated = lax.optimization_barrier(
        (by_role, out_weight, up_weight, down_weight, gated)
    )
    regrouped = lax.all_to_all(gated, "seq", split_axis=0, concat_axis=0, tiled=True)

    tables = {name: jnp.asarray(table) for name, table in transform_tables(length).items()}
    padded = tables["turn"].shape[1]
    rows = length // LANES
    filters = filt_mid.shape[0]
    spectrum, own_taps, own_direct, gate_taps = call(
        functools.partial(filter_kernel, length=length, own=own, group=own),
        "c" * 10,
        (VMEM,) * 4,
        (
            pltpu.HBM((own * padded, 2 * LANES), F32),
            pltpu.VMEM((KSHORT, 8, LANES), F32),
            pltpu.VMEM((own, LANES), F32),
            pltpu.VMEM((KSHORT, width), F32),
        ),
        [
            pltpu.VMEM((own * rows, LANES), F32),
            pltpu.VMEM((width, filters), F32),
            pltpu.VMEM((width, 8), F32),
            pltpu.VMEM((32, filters), F32),
        ],
        24,
        filt_in, filt_bias[None, :], filt_mid, filt_out, decay_rate[None, :], conv_bias[None, :],
        short_weight, tables["turn"], tables["square"], tables["forward3"],
    )
    places = pieces if share % LANES == 0 else 1
    kept_tables = [tables[name] for name in ("turn", "square", "forward2", "inverse3")]
    convolved, side = call(
        functools.partial(
            convolve_kernel, length=length, own=own, own_rows=own_rows, group=own, tokens=tokens, places=places
        ),
        "vvvv" + "h" * 5,
        (HBM, VMEM),
        (pltpu.HBM((places * groups, own, tokens // places), BF16), shape_of((8, width), F32)),
        [
            pltpu.VMEM((own * rows, LANES), F32),
            pltpu.VMEM((own * rows, LANES), F32),
            pltpu.VMEM((places * groups, own, tokens // places), BF16),
            *(pltpu.VMEM(array.shape, array.dtype) for array in (spectrum, *kept_tables)),
            pltpu.SemaphoreType.DMA((5,)),
            pltpu.SemaphoreType.DMA((2,)),
        ],
        40,
        regrouped, own_taps, own_direct, gate_taps, spectrum, *kept_tables,
    )
    if places != pieces:
        convolved = jnp.transpose(convolved.reshape(groups, own, pieces, share), (0, 2, 1, 3))
        convolved = convolved.reshape(groups * pieces, own, share)
    returned = lax.all_to_all(convolved, ("seq", "chan"), split_axis=0, concat_axis=0, tiled=True)
    returned = returned.reshape(groups, pieces, own, share)
    if own % 16:
        returned = jnp.transpose(returned, (1, 0, 2, 3)).reshape(1, pieces, width, share)

    mix_weights = all_turned(out_weight)
    up_weights = all_turned(up_weight)
    down_weights = all_turned(down_weight)
    rest = 64
    gate, mix_kept = call(
        functools.partial(gate_kernel, pieces=pieces, share=share, width=width, rest=rest),
        "c" + "v" * pieces + "h" * (2 * pieces),
        (VMEM, VMEM),
        (pltpu.VMEM((pieces, width, share), F32), pltpu.VMEM((model - rest, model), BF16)),
        [
            pltpu.VMEM((pieces, model, width), BF16),
            pltpu.VMEM((pieces, share + HALO, width), BF16),
            pltpu.VMEM((share + HALO, width), F32),
            pltpu.SemaphoreType.DMA((pieces,)),
            pltpu.SemaphoreType.DMA((pieces,)),
        ],
        16,
        normed, *all_turned(side), *all_turned(by_role), *mix_weights,
    )
    units = up_weight.shape[1]
    block = min(512, units)
    results = call(
        functools.partial(tail_kernel, pieces=pieces, share=share, width=width, block=block, rest=rest),
        "vvvch" + "h" * (1 + 2 * pieces),
        (VMEM,) * pieces,
        tuple(shape_of((share, width), BF16) for p in range(pieces)),
        [
            pltpu.VMEM((share, model), F32),
            pltpu.VMEM((pieces, share, width), BF16),
            pltpu.VMEM((rest, model), BF16),
            pltpu.VMEM((pieces, model, units), BF16),
            pltpu.VMEM((pieces, units, model), BF16),
            pltpu.SemaphoreType.DMA((2,)),
            pltpu.SemaphoreType.DMA((pieces, units // block)),
            pltpu.SemaphoreType.DMA((pieces, units // block)),
        ],
        44,
        returned, gate, mix_kept, gain_second[None, :], my_rows, mix_weights[-1], *up_weights, *down_weights,
    )
    received = [results[0]] + [
        lax.ppermute(results[p], "chan", [(i, (i + p) % pieces) for i in range(pieces)])
        for p in range(1, pieces)
    ]
    return call(
        functools.partial(join_kernel, pieces=pieces, share=share),
        "v" * pieces,
        HBM,
        pltpu.HBM((tokens, width), BF16),
        [pltpu.SemaphoreType.DMA((pieces,))],
        8,
        *received,
    )


def solution(mesh):
    placed = (
        P("seq", "chan"),
        P(),
        P(None, None, "chan"),
        P(None, None, "chan"),
        P(),
        P(),
        P(),
        P(None, "chan"),
        P("chan"),
        P("chan"),
        P("chan", None),
        P(),
        P(None, "chan"),
        P("chan", None),
    )
    return jax.shard_map(
        per_device, mesh=mesh, in_specs=placed, out_specs=P("seq", "chan"), check_vma=False
    )
```

```python
import functools

import jax
import jax.numpy as jnp
import ml_dtypes
import numpy as np
from jax import lax
from jax.experimental import pallas as pl
from jax.experimental.pallas import tpu as pltpu
from jax.sharding import PartitionSpec as P

BANDS = 12
KSHORT = 3
LANES = 128
HALO = 16
AHEAD = 4
EPS = 1e-05
PI_HIGH = 3.140625
PI_LOW = 9.67653589793e-4
F32 = jnp.float32
BF16 = jnp.bfloat16
VMEM_BYTES = 60 * 1024 * 1024


def matmul(left, right):
    return jnp.dot(left, right, preferred_element_type=F32)


def split_parts(values):
    high = values.astype(BF16)
    return high, (values - high.astype(F32)).astype(BF16)


def split_table(table):
    high = table.astype(np.float32).astype(ml_dtypes.bfloat16)
    low = (table - high.astype(np.float64)).astype(np.float32).astype(ml_dtypes.bfloat16)
    return high, low


def transform_tables(length):
    rows = length // LANES
    period = 2 * rows
    full = 2 * length
    kept = rows + 1
    padded = -(-kept // 8) * 8
    k2 = np.arange(padded)
    valid = (k2 < kept).astype(np.float64)[:, None]
    n2 = np.arange(rows)
    n1 = np.arange(LANES)
    first = 2 * np.pi / period * (k2[:, None] * n2[None, :] % period)
    forward = np.concatenate([np.cos(first) * valid, -np.sin(first) * valid], 0)
    weight = np.where((k2 == 0) | (k2 == rows), 1.0, 2.0)[:, None] * valid
    inverse = np.concatenate([np.cos(first) * weight, -np.sin(first) * weight], 0).T
    turn = 2 * np.pi / full * (k2[:, None] * n1[None, :] % full)
    second = 2 * np.pi / LANES * (n1[:, None] * n1[None, :] % LANES)
    cos2, sin2 = np.cos(second), np.sin(second)
    mid = np.concatenate(
        [np.concatenate([cos2, -sin2], 1), np.concatenate([sin2, cos2], 1)], 0
    )
    back = np.concatenate(
        [np.concatenate([cos2, sin2], 1), np.concatenate([-sin2, cos2], 1)], 0
    ) / full
    f_high, f_low = split_table(forward)
    i_high, i_low = split_table(inverse)
    f_high, f_low = split_table(forward)
    i_high, i_low = split_table(inverse)
    return {
        "turn": np.tile(np.stack([np.cos(turn), np.sin(turn)]), (1, 1, 2)).astype(np.float32),
        "square": np.stack([*split_table(mid), *split_table(back)]),
        "forward3": np.concatenate([f_high, f_high, f_low], 1),
        "forward2": np.concatenate([f_high, f_low], 1),
        "inverse3": np.concatenate([i_high, i_high, i_low], 1),
    }


def sine(values):
    count = jnp.floor(values * (1.0 / np.pi) + 0.5)
    rest = (values - count * PI_HIGH) - count * PI_LOW
    half = count * 0.5
    sign = 1.0 - 4.0 * (half - jnp.floor(half))
    return sign * sine_poly(rest)


def sine_poly(rest):
    square = rest * rest
    poly = -2.5052108385441720e-08
    poly = poly * square + 2.7557319223985893e-06
    poly = poly * square - 1.9841269841269841e-04
    poly = poly * square + 8.3333333333333333e-03
    poly = poly * square - 1.6666666666666667e-01
    return rest + rest * square * poly


def sine_turns(turns):
    count = jnp.floor(turns * 2.0 + 0.5)
    rest = (turns - count * 0.5) * (2.0 * np.pi)
    half = count * 0.5
    sign = 1.0 - 4.0 * (half - jnp.floor(half))
    return sign * sine_poly(rest)


def rows_to_spectrum(load_pair, group, table, turn_cos, turn_sin, mid_high, mid_low, padded):
    stacked = []
    for pair in range(group // 2):
        first = matmul(table, load_pair(pair))
        real, imag = first[:padded], first[padded:]
        turned_real = real * turn_cos + imag * turn_sin
        turned_imag = imag * turn_cos - real * turn_sin
        for side in range(2):
            lanes = slice(side * LANES, (side + 1) * LANES)
            stacked.append(jnp.concatenate([turned_real[:, lanes], turned_imag[:, lanes]], 1))
    if mid_low is None:
        return matmul(jnp.concatenate(stacked, 0).astype(BF16), mid_high)
    high, low = split_parts(jnp.concatenate(stacked, 0))
    return matmul(high, mid_high) + matmul(low, mid_high) + matmul(high, mid_low)


def project_kernel(
    *refs, pieces, tokens, width, own, own_rows, share
):
    x_refs, refs = refs[:pieces], refs[pieces:]
    gain_ref, taps_ref, w_hbm, normed_hbm, rows_hbm, out_hbm, refs = *refs[:6], refs[6:]
    w_ref, proj_ref, block_ref, normed_ref, w_sems, out_sems, normed_sem, row_sems = refs
    me = lax.axis_index("chan")
    places = [lax.rem(me + p, pieces) for p in range(pieces)]
    total = pieces * width
    loads = [pltpu.make_async_copy(w_hbm.at[(role + 1) % 3], w_ref.at[role], w_sems.at[role]) for role in range(3)]
    for load in loads:
        load.start()
    chunk = 128
    for start in range(0, tokens, chunk):
        values = [ref[start : start + chunk, :].astype(F32) for ref in x_refs]
        mean = sum(jnp.sum(v, axis=1, keepdims=True) for v in values) / total
        centered = [v - mean for v in values]
        spread = sum(jnp.sum(c * c, axis=1, keepdims=True) for c in centered) / total
        scale = lax.rsqrt(spread + EPS)
        for p in range(pieces):
            gain = gain_ref[places[p]]
            normed_ref[p, start : start + chunk, :] = (centered[p] * scale * gain).astype(BF16)
    mine = pl.ds(pl.multiple_of(me * share, 16), share)
    keeps = [pltpu.make_async_copy(normed_ref, normed_hbm, normed_sem)]
    for p in range(pieces):
        keeps.append(pltpu.make_async_copy(x_refs[p].at[mine], rows_hbm.at[p], row_sems.at[p]))
    for keep in keeps:
        keep.start()
    step = min(width, 512)
    per_step = step // own
    parts = tokens // LANES
    proj_ref[:, :8, :] = jnp.zeros((2, 8, step), F32)
    for load in loads[:2]:
        load.wait()
    stores = []
    for col in range(0, width, step):
        cols = slice(col, col + step)
        for role in range(2):
            sums = 0.0
            for p in range(pieces):
                rows = pl.ds(pl.multiple_of(places[p] * width, width), width)
                sums = sums + matmul(normed_ref[p], w_ref[role, rows, cols])
            proj_ref[role, 8:, :] = sums.astype(BF16).astype(F32)
        shorted = []
        for role in range(2):
            value = taps_ref[0, role + 1 : role + 2, cols] * proj_ref[role, 8 : 8 + tokens, :]
            for lag in range(1, KSHORT):
                value = (
                    value
                    + taps_ref[lag, role + 1 : role + 2, cols] * proj_ref[role, 8 - lag : 8 - lag + tokens, :]
                )
            shorted.append(value)
        gated = (shorted[1] * shorted[0]).T
        if col == 0:
            loads[2].wait()
            last = 0.0
            for p in range(pieces):
                rows = pl.ds(pl.multiple_of(places[p] * width, width), width)
                last = last + matmul(normed_ref[p, tokens - HALO :, :], w_ref[2, rows, :])
            last = last.astype(BF16).astype(F32)
            spread_last = [
                last[row : row + 1, lane : lane + LANES]
                for row in (HALO - 2, HALO - 1)
                for lane in range(0, width, LANES)
            ]
            spread_last = jnp.concatenate(spread_last + [jnp.zeros((8 - len(spread_last), LANES), F32)][: len(spread_last) < 8], 0)
        edges = jnp.concatenate(
            [
                proj_ref[0, 8:10, :],
                proj_ref[0, 6 + tokens : 8 + tokens, :],
                proj_ref[1, 8:10, :],
                proj_ref[1, 6 + tokens : 8 + tokens, :],
            ],
            0,
        )
        first = col // own
        for d in range(per_step):
            for part in range(parts):
                block_ref[first + d, part * own_rows : part * own_rows + own, :] = gated[
                    d * own : (d + 1) * own, part * LANES : (part + 1) * LANES
                ].astype(BF16)
            block_edges = jnp.concatenate([edges[:, d * own : (d + 1) * own], jnp.zeros((8, LANES - own), F32)], 1)
            block_ref[first + d, parts * own_rows :, :] = jnp.concatenate([block_edges, spread_last], 0).astype(BF16)
        targets = pl.ds(first, per_step)
        store = pltpu.make_async_copy(block_ref.at[targets], out_hbm.at[targets], out_sems.at[col // step])
        store.start()
        stores.append(store)
    for store in stores:
        store.wait()
    for keep in keeps:
        keep.wait()


def gate_kernel(normed_ref, *refs, pieces, share, width, rest):
    side_refs, refs = refs[:pieces], refs[pieces:]
    w_hbm, refs = refs[:pieces], refs[pieces:]
    mix_hbm, (gate_ref, mix_ref, w_ref, rows_ref, proj_ref, w_sems, mix_sems) = refs[:pieces], refs[pieces:]
    fetches = []
    for p in range(pieces):
        size = width - rest if p == pieces - 1 else width
        fetches.append(
            pltpu.make_async_copy(
                mix_hbm[p].at[pl.ds(0, size)], mix_ref.at[pl.ds(p * width, size)], mix_sems.at[p]
            )
        )
    loads = [pltpu.make_async_copy(w_hbm[p].at[0], w_ref.at[p], w_sems.at[p]) for p in range(pieces)]
    for load in loads + fetches:
        load.start()
    me = lax.axis_index("chan")
    places = [lax.rem(me + p, pieces) for p in range(pieces)]
    mine = pl.ds(pl.multiple_of(me * share, 16), share)
    before = pl.ds(pl.multiple_of(jnp.maximum(me * share - HALO, 0), 16), HALO)
    for p in range(pieces):
        rows_ref[p, HALO:, :] = normed_ref[p, mine, :]
        rows_ref[p, :HALO, :] = normed_ref[p, before, :]
    for load in loads:
        load.wait()
    for out in range(pieces):
        sums = 0.0
        for p in range(pieces):
            rows = pl.ds(pl.multiple_of(places[p] * width, width), width)
            sums = sums + matmul(rows_ref[p], w_ref[out, rows, :])
        proj_ref[...] = sums.astype(BF16).astype(F32)
        proj_ref[HALO - 2 : HALO, :] = jnp.where(
            me == 0, side_refs[out][KSHORT : KSHORT + 2, :], proj_ref[HALO - 2 : HALO, :]
        )
        value = side_refs[out][0:1, :] * proj_ref[HALO : HALO + share, :]
        for lag in range(1, KSHORT):
            value = value + side_refs[out][lag : lag + 1, :] * proj_ref[HALO - lag : HALO - lag + share, :]
        gate_ref[out] = value.T
    for fetch in fetches:
        fetch.wait()


def filter_kernel(
    in_ref, bias_ref, mid_w_ref, out_w_ref, decay_ref, direct_ref, taps_ref,
    turn_ref, square_ref, forward_ref, spectrum_ref, own_taps_ref, own_direct_ref, gate_taps_ref,
    response_ref, columns_ref, scalars_ref, in_pad_ref, *, length, own, group
):
    padded = turn_ref.shape[1]
    seq_place = lax.axis_index("seq")
    width = out_w_ref.shape[1]
    feats = in_pad_ref.shape[0]
    in_pad_ref[...] = jnp.zeros(in_pad_ref.shape, F32)
    in_pad_ref[: in_ref.shape[0], :] = in_ref[...].astype(F32)
    in_columns = in_pad_ref[...].T.astype(BF16)
    mid_columns = mid_w_ref[...].astype(F32).T.astype(BF16)
    bias = jnp.broadcast_to(bias_ref[...], (8, bias_ref.shape[1])).T[:, :1]
    columns_ref[...] = out_w_ref[...].astype(F32).T
    scalars_ref[...] = jnp.concatenate(
        [jnp.broadcast_to(decay_ref[...], (4, width)), jnp.broadcast_to(direct_ref[...], (4, width))], 0
    ).T
    mine = pl.ds(seq_place * own, own)
    out_columns = columns_ref[mine, :].astype(BF16)
    decay = scalars_ref[mine, 0:1]
    own_direct_ref[...] = jnp.broadcast_to(scalars_ref[mine, 4:5], (own, LANES))
    shift = lax.rem(width - seq_place * own, width)
    for lag in range(KSHORT):
        own_taps = pltpu.roll(jnp.concatenate([taps_ref[lag], jnp.zeros((5, width), F32)], 0), shift, 1)
        own_taps_ref[lag] = own_taps[:, :LANES]
        gate_taps_ref[lag : lag + 1, :] = taps_ref[lag, 0:1, :]
    rows = length // LANES
    chunk = min(1024, length)
    row_ids = lax.broadcasted_iota(jnp.int32, (feats, chunk), 0)
    band = jnp.where(row_ids > BANDS, row_ids - (BANDS + 1), row_ids - 1)
    band = jnp.clip(band, 0, BANDS - 1)
    quarter = jnp.where(row_ids <= BANDS, 0.25, 0.0)
    for start in range(0, length, chunk):
        places = lax.broadcasted_iota(jnp.int32, (feats, chunk), 1) + start
        phase = lax.shift_left(places, band) & (length - 1)
        turns = phase.astype(F32) * (1.0 / length)
        waves = sine_turns(turns + quarter)
        features = jnp.where(
            row_ids == 0,
            places.astype(F32) / length,
            jnp.where(row_ids <= 2 * BANDS, waves, 0.0),
        ).astype(BF16)
        first = sine(matmul(in_columns, features) + bias).astype(BF16)
        second = sine(matmul(mid_columns, first)).astype(BF16)
        ramp = (lax.broadcasted_iota(jnp.int32, (1, chunk), 1) + start).astype(F32) / length
        response = matmul(out_columns, second) * jnp.exp(-decay * ramp)
        for part in range(chunk // LANES):
            row = start // LANES + part
            response_ref[pl.ds(row, own, stride=rows), :] = response[:, part * LANES : (part + 1) * LANES]

    def one_group(step, carry):
        def load_pair(pair):
            base = (step * group + 2 * pair) * rows
            both = [
                response_ref[pl.ds(pl.multiple_of(base + side * rows, 8), rows), :] for side in range(2)
            ]
            high, low = split_parts(jnp.concatenate(both, 1))
            return jnp.concatenate([high, low, high], 0)

        spectrum = rows_to_spectrum(
            load_pair, group, forward_ref[...], turn_ref[0], turn_ref[1], square_ref[0], square_ref[1], padded
        )
        spectrum_ref[pl.ds(pl.multiple_of(step * group * padded, 8), group * padded), :] = spectrum
        return carry

    if own == group:
        one_group(0, 0)
    else:
        lax.fori_loop(0, own // group, one_group, 0)


def convolve_kernel(
    x_ref, taps_ref, direct_ref, gate_taps_ref, spectrum_hbm, turn_hbm, square_hbm, forward_hbm, inverse_hbm, out_hbm, side_ref,
    signal_ref, result_ref, out_ref, spectrum_ref, turn_ref, square_ref, forward_ref, inverse_ref,
    load_sems, out_sems, *, length, own, own_rows, group, tokens, places
):
    padded = turn_ref.shape[1]
    sources = (forward_hbm, turn_hbm, square_hbm, inverse_hbm, spectrum_hbm)
    targets = (forward_ref, turn_ref, square_ref, inverse_ref, spectrum_ref)
    loads = [pltpu.make_async_copy(s, t, load_sems.at[k]) for k, (s, t) in enumerate(zip(sources, targets))]
    for load in loads:
        load.start()
    rows = length // LANES
    per_block = tokens // LANES
    blocks = length // tokens
    seq_place = lax.axis_index("seq")
    width = side_ref.shape[1]
    count = width // LANES
    before = x_ref[jnp.maximum(seq_place - 1, 0), per_block * own_rows :, :].astype(F32)
    before = jnp.where(seq_place > 0, before, 0.0)
    side_ref[...] = jnp.zeros(side_ref.shape, F32)
    side_ref[:KSHORT, :] = gate_taps_ref[...]
    for k in range(2 * count):
        row, lanes = KSHORT + k // count, slice(k % count * LANES, (k % count + 1) * LANES)
        side_ref[row : row + 1, lanes] = before[8 + k : 9 + k, :]
    lane = lax.broadcasted_iota(jnp.int32, (own, LANES), 1)
    fixes = []
    last = [jnp.zeros((2, LANES), F32)] * 2
    for block in range(blocks):
        edge = x_ref[block, per_block * own_rows :, :].astype(F32)
        starts = []
        for role in range(2):
            here, before = edge[4 * role : 4 * role + 2], last[role]
            two_back = jnp.concatenate([before[1:2], here[0:1]], 0)
            starts.append(
                taps_ref[0, role + 1 : role + 2, :] * here
                + taps_ref[1, role + 1 : role + 2, :] * two_back
                + taps_ref[2, role + 1 : role + 2, :] * before
            )
            last[role] = edge[4 * role + 2 : 4 * role + 4]
        fixes.append(starts[1] * starts[0])
    fixed = jnp.concatenate(fixes, 0)
    if 2 * blocks < LANES:
        fixed = jnp.concatenate([fixed, jnp.zeros((LANES - 2 * blocks, LANES), F32)], 0)
    fixed = fixed.T[:own]
    for row in range(rows):
        block, part = divmod(row, per_block)
        values = x_ref[block, part * own_rows : part * own_rows + own, :].astype(F32)
        if part == 0:
            values = jnp.where(lane == 0, fixed[:, 2 * block : 2 * block + 1], values)
            values = jnp.where(lane == 1, fixed[:, 2 * block + 1 : 2 * block + 2], values)
        signal_ref[pl.ds(row, own, stride=rows), :] = values
    for load in loads[:3]:
        load.wait()
    turn_cos, turn_sin = turn_ref[0], turn_ref[1]

    def one_group(step, carry):
        def load_pair(pair):
            base = (step * group + 2 * pair) * rows
            both = [
                signal_ref[pl.ds(pl.multiple_of(base + side * rows, 8), rows), :] for side in range(2)
            ]
            values = jnp.concatenate(both, 1).astype(BF16)
            return jnp.concatenate([values, values], 0)

        signal = rows_to_spectrum(
            load_pair, group, forward_ref[...], turn_cos, turn_sin, square_ref[0], None, padded
        )
        if own == group:
            for load in loads[3:]:
                load.wait()
        other = spectrum_ref[pl.ds(pl.multiple_of(step * group * padded, 8), group * padded), :]
        s_real, s_imag = signal[:, :LANES], signal[:, LANES:]
        f_real, f_imag = other[:, :LANES], other[:, LANES:]
        product = jnp.concatenate(
            [s_real * f_real - s_imag * f_imag, s_real * f_imag + s_imag * f_real], 1
        )
        mixed = matmul(product.astype(BF16), square_ref[2])
        for pair in range(group // 2):
            first = mixed[2 * pair * padded : (2 * pair + 1) * padded]
            second = mixed[(2 * pair + 1) * padded : (2 * pair + 2) * padded]
            real = jnp.concatenate([first[:, :LANES], second[:, :LANES]], 1)
            imag = jnp.concatenate([first[:, LANES:], second[:, LANES:]], 1)
            turned = jnp.concatenate(
                [real * turn_cos - imag * turn_sin, imag * turn_cos + real * turn_sin], 0
            )
            t_high, t_low = split_parts(turned)
            values = matmul(inverse_ref[...], jnp.concatenate([t_high, t_low, t_high], 0))
            base = (step * group + 2 * pair) * rows
            for side in range(2):
                result_ref[pl.ds(pl.multiple_of(base + side * rows, 8), rows), :] = values[
                    :, side * LANES : (side + 1) * LANES
                ]
        return carry

    if own == group:
        one_group(0, 0)
    else:
        for load in loads[3:]:
            load.wait()
        lax.fori_loop(0, own // group, one_group, 0)
    bias = direct_ref[...]
    share_rows = per_block // places
    blocks = length // tokens
    stores, half = [], max(blocks // 2, 1)
    for row in range(rows):
        block, part = divmod(row, per_block)
        place, side = divmod(part, share_rows)
        values = result_ref[pl.ds(row, own, stride=rows), :]
        values = values + bias * signal_ref[pl.ds(row, own, stride=rows), :]
        target = block * places + place
        out_ref[target, :, side * LANES : (side + 1) * LANES] = values.astype(BF16)
        if part == per_block - 1 and (block + 1) % half == 0:
            span = pl.ds((block + 1 - half) * places, half * places)
            store = pltpu.make_async_copy(out_ref.at[span], out_hbm.at[span], out_sems.at[len(stores)])
            store.start()
            stores.append(store)
    for store in stores:
        store.wait()


def gelu(values):
    return values * (lax.erf(values * np.float32(0.5**0.5)) + 1.0) * 0.5


def tail_kernel(
    z_ref, gate_ref, mix_ref, gain_ref, rows_hbm, *refs, pieces, share, width, block, rest
):
    mix_hbm, refs = refs[0], refs[1:]
    up_hbm, refs = refs[:pieces], refs[pieces:]
    down_hbm, refs = refs[:pieces], refs[pieces:]
    out_refs, refs = refs[:pieces], refs[pieces:]
    sums_ref, rows_ref, rest_ref, up_ref, down_ref, first_sems, up_sems, down_sems = refs
    total = pieces * width
    steps = up_ref.shape[2] // block
    count = pieces * steps
    firsts = [
        pltpu.make_async_copy(mix_hbm.at[pl.ds(width - rest, rest)], rest_ref, first_sems.at[0]),
        pltpu.make_async_copy(rows_hbm, rows_ref, first_sems.at[1]),
    ]
    ups, downs = [], []
    for p in range(pieces):
        for k in range(steps):
            cols = pl.ds(k * block, block)
            ups.append(pltpu.make_async_copy(up_hbm[p].at[:, cols], up_ref.at[p, :, cols], up_sems.at[p, k]))
            downs.append(pltpu.make_async_copy(down_hbm[p].at[cols], down_ref.at[p, cols], down_sems.at[p, k]))
    copies = list(firsts)
    for k in range(count + 2):
        copies += ups[k : k + 1]
        if k >= 2:
            copies.append(downs[k - 2])
    started, waited = [0], [0]

    def start_until(limit):
        while started[0] < min(limit, len(copies)):
            copies[started[0]].start()
            started[0] += 1

    def next_copy():
        start_until(waited[0] + AHEAD)
        copies[waited[0]].wait()
        waited[0] += 1

    start_until(AHEAD)
    me = lax.axis_index("chan")
    places = [lax.rem(me + p, pieces) for p in range(pieces)]
    dims = (((0,), (0,)), ((), ()))
    sums = 0.0
    for p in range(pieces):
        mixed = (z_ref[:, places[p]].reshape(width, share).astype(F32) * gate_ref[p]).astype(BF16)
        size = width - rest if p == pieces - 1 else width
        kept = mix_ref[p * width : p * width + size, :]
        sums = sums + lax.dot_general(mixed[:size], kept, dims, preferred_element_type=F32)
    next_copy()
    sums = sums + lax.dot_general(mixed[width - rest :], rest_ref[...], dims, preferred_element_type=F32)
    sums_ref[...] = sums
    next_copy()
    for p in range(pieces):
        cols = pl.ds(pl.multiple_of(places[p] * width, LANES), width)
        residual = rows_ref[p].astype(F32) + sums_ref[:, cols]
        sums_ref[:, cols] = residual.astype(BF16).astype(F32)
    values = sums_ref[...]
    mean = jnp.sum(values, axis=1, keepdims=True) / total
    centered = values - mean
    spread = jnp.sum(centered * centered, axis=1, keepdims=True) / total
    normed = (centered * lax.rsqrt(spread + EPS) * gain_ref[...]).astype(BF16)
    lifted = hidden = None
    for k in range(count + 2):
        new_lifted = new_hidden = None
        if k < count:
            next_copy()
            p, part = divmod(k, steps)
            new_lifted = matmul(normed, up_ref[p, :, part * block : (part + 1) * block])
        if lifted is not None:
            new_hidden = gelu(lifted).astype(BF16)
        if k >= 2:
            next_copy()
            p, part = divmod(k - 2, steps)
            sums_ref[...] += matmul(hidden, down_ref[p, part * block : (part + 1) * block, :])
        lifted, hidden = new_lifted, new_hidden
    for p in range(pieces):
        cols = pl.ds(pl.multiple_of(places[p] * width, LANES), width)
        out_refs[p][...] = sums_ref[:, cols].astype(BF16)


def join_kernel(*refs, pieces, share):
    out_hbm, sems = refs[pieces:]
    me = lax.axis_index("chan")
    copies = []
    for p in range(pieces):
        start = lax.rem(me + pieces - p, pieces) * share
        rows = pl.ds(pl.multiple_of(start, 16), share)
        copies.append(pltpu.make_async_copy(refs[p], out_hbm.at[rows], sems.at[p]))
    for copy in copies:
        copy.start()
    for copy in copies:
        copy.wait()


HBM = pl.BlockSpec(memory_space=pltpu.HBM)
VMEM = pl.BlockSpec(memory_space=pltpu.VMEM)


def call(kernel, in_specs, out_specs, out_shape, scratch, megabytes, *args):
    kinds = {"h": HBM, "v": VMEM, "c": VMEM}
    spaces = {"h": pltpu.HBM, "v": pltpu.VMEM, "c": pltpu.HBM}
    placed = [
        pltpu.with_memory_space_constraint(arg, spaces[kind])
        for kind, arg in zip(in_specs, args, strict=True)
    ]
    return pl.pallas_call(
        kernel,
        in_specs=[kinds[kind] for kind in in_specs],
        out_specs=out_specs,
        out_shape=out_shape,
        scratch_shapes=scratch,
        compiler_params=pltpu.CompilerParams(vmem_limit_bytes=megabytes * 1024 * 1024),
    )(*placed)


def shape_of(shape, dtype):
    return jax.ShapeDtypeStruct(shape, dtype)


def per_device(
    layer_input, gain_first, in_weight, short_weight, filt_in, filt_bias, filt_mid, filt_out,
    decay_rate, conv_bias, out_weight, gain_second, up_weight, down_weight,
):
    tokens, width = layer_input.shape
    pieces = lax.axis_size("chan")
    groups = lax.axis_size("seq")
    model = pieces * width
    length = tokens * groups
    share = tokens // pieces
    own = width // groups
    own_rows = -(-own // 16) * 16
    block_rows = tokens // LANES * own_rows + 16

    def turned(array, by):
        if by == 0:
            return array
        return lax.ppermute(array, "chan", [(i, (i - by) % pieces) for i in range(pieces)])

    def all_turned(array):
        return [turned(array, p) for p in range(pieces)]

    x_pieces = all_turned(layer_input)
    by_role = jnp.transpose(in_weight, (1, 0, 2))
    step = min(width, 512)
    normed, my_rows, gated = call(
        functools.partial(
            project_kernel, pieces=pieces, tokens=tokens, width=width, own=own, own_rows=own_rows, share=share
        ),
        "c" + "v" * (pieces - 1) + "cch",
        (HBM, HBM, HBM),
        (
            pltpu.HBM((pieces, tokens, width), BF16),
            pltpu.HBM((pieces, share, width), BF16),
            pltpu.HBM((groups, block_rows, LANES), BF16),
        ),
        [
            pltpu.VMEM((3, model, width), BF16),
            pltpu.VMEM((2, tokens + 8, step), F32),
            pltpu.VMEM((groups, block_rows, LANES), BF16),
            pltpu.VMEM((pieces, tokens, width), BF16),
            pltpu.SemaphoreType.DMA((3,)),
            pltpu.SemaphoreType.DMA((width // step,)),
            pltpu.SemaphoreType.DMA,
            pltpu.SemaphoreType.DMA((pieces,)),
        ],
        20,
        *x_pieces, gain_first.reshape(pieces, 1, width), short_weight, by_role,
    )
    by_role, out_weight, up_weight, down_weight, gated = lax.optimization_barrier(
        (by_role, out_weight, up_weight, down_weight, gated)
    )
    regrouped = lax.all_to_all(gated, "seq", split_axis=0, concat_axis=0, tiled=True)

    tables = {name: jnp.asarray(table) for name, table in transform_tables(length).items()}
    padded = tables["turn"].shape[1]
    rows = length // LANES
    filters = filt_mid.shape[0]
    spectrum, own_taps, own_direct, gate_taps = call(
        functools.partial(filter_kernel, length=length, own=own, group=own),
        "c" * 10,
        (VMEM,) * 4,
        (
            pltpu.HBM((own * padded, 2 * LANES), F32),
            pltpu.VMEM((KSHORT, 8, LANES), F32),
            pltpu.VMEM((own, LANES), F32),
            pltpu.VMEM((KSHORT, width), F32),
        ),
        [
            pltpu.VMEM((own * rows, LANES), F32),
            pltpu.VMEM((width, filters), F32),
            pltpu.VMEM((width, 8), F32),
            pltpu.VMEM((32, filters), F32),
        ],
        24,
        filt_in, filt_bias[None, :], filt_mid, filt_out, decay_rate[None, :], conv_bias[None, :],
        short_weight, tables["turn"], tables["square"], tables["forward3"],
    )
    places = pieces if share % LANES == 0 else 1
    kept_tables = [tables[name] for name in ("turn", "square", "forward2", "inverse3")]
    convolved, side = call(
        functools.partial(
            convolve_kernel, length=length, own=own, own_rows=own_rows, group=own, tokens=tokens, places=places
        ),
        "vvvv" + "h" * 5,
        (HBM, VMEM),
        (pltpu.HBM((places * groups, own, tokens // places), BF16), shape_of((8, width), F32)),
        [
            pltpu.VMEM((own * rows, LANES), F32),
            pltpu.VMEM((own * rows, LANES), F32),
            pltpu.VMEM((places * groups, own, tokens // places), BF16),
            *(pltpu.VMEM(array.shape, array.dtype) for array in (spectrum, *kept_tables)),
            pltpu.SemaphoreType.DMA((5,)),
            pltpu.SemaphoreType.DMA((2,)),
        ],
        40,
        regrouped, own_taps, own_direct, gate_taps, spectrum, *kept_tables,
    )
    if places != pieces:
        convolved = jnp.transpose(convolved.reshape(groups, own, pieces, share), (0, 2, 1, 3))
        convolved = convolved.reshape(groups * pieces, own, share)
    returned = lax.all_to_all(convolved, ("seq", "chan"), split_axis=0, concat_axis=0, tiled=True)
    returned = returned.reshape(groups, pieces, own, share)
    if own % 16:
        returned = jnp.transpose(returned, (1, 0, 2, 3)).reshape(1, pieces, width, share)

    mix_weights = all_turned(out_weight)
    up_weights = all_turned(up_weight)
    down_weights = all_turned(down_weight)
    rest = 64
    gate, mix_kept = call(
        functools.partial(gate_kernel, pieces=pieces, share=share, width=width, rest=rest),
        "c" + "v" * pieces + "h" * (2 * pieces),
        (VMEM, VMEM),
        (pltpu.VMEM((pieces, width, share), F32), pltpu.VMEM((model - rest, model), BF16)),
        [
            pltpu.VMEM((pieces, model, width), BF16),
            pltpu.VMEM((pieces, share + HALO, width), BF16),
            pltpu.VMEM((share + HALO, width), F32),
            pltpu.SemaphoreType.DMA((pieces,)),
            pltpu.SemaphoreType.DMA((pieces,)),
        ],
        16,
        normed, *all_turned(side), *all_turned(by_role), *mix_weights,
    )
    units = up_weight.shape[1]
    block = min(1024, units)
    results = call(
        functools.partial(tail_kernel, pieces=pieces, share=share, width=width, block=block, rest=rest),
        "vvvch" + "h" * (1 + 2 * pieces),
        (VMEM,) * pieces,
        tuple(shape_of((share, width), BF16) for p in range(pieces)),
        [
            pltpu.VMEM((share, model), F32),
            pltpu.VMEM((pieces, share, width), BF16),
            pltpu.VMEM((rest, model), BF16),
            pltpu.VMEM((pieces, model, units), BF16),
            pltpu.VMEM((pieces, units, model), BF16),
            pltpu.SemaphoreType.DMA((2,)),
            pltpu.SemaphoreType.DMA((pieces, units // block)),
            pltpu.SemaphoreType.DMA((pieces, units // block)),
        ],
        44,
        returned, gate, mix_kept, gain_second[None, :], my_rows, mix_weights[-1], *up_weights, *down_weights,
    )
    received = [results[0]] + [
        lax.ppermute(results[p], "chan", [(i, (i + p) % pieces) for i in range(pieces)])
        for p in range(1, pieces)
    ]
    return call(
        functools.partial(join_kernel, pieces=pieces, share=share),
        "v" * pieces,
        HBM,
        pltpu.HBM((tokens, width), BF16),
        [pltpu.SemaphoreType.DMA((pieces,))],
        8,
        *received,
    )


def solution(mesh):
    placed = (
        P("seq", "chan"),
        P(),
        P(None, None, "chan"),
        P(None, None, "chan"),
        P(),
        P(),
        P(),
        P(None, "chan"),
        P("chan"),
        P("chan"),
        P("chan", None),
        P(),
        P(None, "chan"),
        P("chan", None),
    )
    return jax.shard_map(
        per_device, mesh=mesh, in_specs=placed, out_specs=P("seq", "chan"), check_vma=False
    )
```

```python
import functools

import jax
import jax.numpy as jnp
import ml_dtypes
import numpy as np
from jax import lax
from jax.experimental import pallas as pl
from jax.experimental.pallas import tpu as pltpu
from jax.sharding import PartitionSpec as P

BANDS = 12
KSHORT = 3
LANES = 128
HALO = 16
AHEAD = 4
EPS = 1e-05
PI_HIGH = 3.140625
PI_LOW = 9.67653589793e-4
F32 = jnp.float32
BF16 = jnp.bfloat16
VMEM_BYTES = 60 * 1024 * 1024


def matmul(left, right):
    return jnp.dot(left, right, preferred_element_type=F32)


def split_parts(values):
    high = values.astype(BF16)
    return high, (values - high.astype(F32)).astype(BF16)


def split_table(table):
    high = table.astype(np.float32).astype(ml_dtypes.bfloat16)
    low = (table - high.astype(np.float64)).astype(np.float32).astype(ml_dtypes.bfloat16)
    return high, low


def transform_tables(length):
    rows = length // LANES
    period = 2 * rows
    full = 2 * length
    kept = rows + 1
    padded = -(-kept // 8) * 8
    k2 = np.arange(padded)
    valid = (k2 < kept).astype(np.float64)[:, None]
    n2 = np.arange(rows)
    n1 = np.arange(LANES)
    first = 2 * np.pi / period * (k2[:, None] * n2[None, :] % period)
    forward = np.concatenate([np.cos(first) * valid, -np.sin(first) * valid], 0)
    weight = np.where((k2 == 0) | (k2 == rows), 1.0, 2.0)[:, None] * valid
    inverse = np.concatenate([np.cos(first) * weight, -np.sin(first) * weight], 0).T
    turn = 2 * np.pi / full * (k2[:, None] * n1[None, :] % full)
    second = 2 * np.pi / LANES * (n1[:, None] * n1[None, :] % LANES)
    cos2, sin2 = np.cos(second), np.sin(second)
    mid = np.concatenate(
        [np.concatenate([cos2, -sin2], 1), np.concatenate([sin2, cos2], 1)], 0
    )
    back = np.concatenate(
        [np.concatenate([cos2, sin2], 1), np.concatenate([-sin2, cos2], 1)], 0
    ) / full
    f_high, f_low = split_table(forward)
    i_high, i_low = split_table(inverse)
    f_high, f_low = split_table(forward)
    i_high, i_low = split_table(inverse)
    return {
        "turn": np.tile(np.stack([np.cos(turn), np.sin(turn)]), (1, 1, 2)).astype(np.float32),
        "square": np.stack([*split_table(mid), *split_table(back)]),
        "forward3": np.concatenate([f_high, f_high, f_low], 1),
        "forward2": np.concatenate([f_high, f_low], 1),
        "inverse3": np.concatenate([i_high, i_high, i_low], 1),
    }


def sine(values):
    count = jnp.floor(values * (1.0 / np.pi) + 0.5)
    rest = (values - count * PI_HIGH) - count * PI_LOW
    half = count * 0.5
    sign = 1.0 - 4.0 * (half - jnp.floor(half))
    return sign * sine_poly(rest)


def sine_poly(rest):
    square = rest * rest
    poly = -2.5052108385441720e-08
    poly = poly * square + 2.7557319223985893e-06
    poly = poly * square - 1.9841269841269841e-04
    poly = poly * square + 8.3333333333333333e-03
    poly = poly * square - 1.6666666666666667e-01
    return rest + rest * square * poly


def sine_turns(turns):
    count = jnp.floor(turns * 2.0 + 0.5)
    rest = (turns - count * 0.5) * (2.0 * np.pi)
    half = count * 0.5
    sign = 1.0 - 4.0 * (half - jnp.floor(half))
    return sign * sine_poly(rest)


def rows_to_spectrum(load_pair, group, table, turn_cos, turn_sin, mid_high, mid_low, padded):
    stacked = []
    for pair in range(group // 2):
        first = matmul(table, load_pair(pair))
        real, imag = first[:padded], first[padded:]
        turned_real = real * turn_cos + imag * turn_sin
        turned_imag = imag * turn_cos - real * turn_sin
        for side in range(2):
            lanes = slice(side * LANES, (side + 1) * LANES)
            stacked.append(jnp.concatenate([turned_real[:, lanes], turned_imag[:, lanes]], 1))
    if mid_low is None:
        return matmul(jnp.concatenate(stacked, 0).astype(BF16), mid_high)
    high, low = split_parts(jnp.concatenate(stacked, 0))
    return matmul(high, mid_high) + matmul(low, mid_high) + matmul(high, mid_low)


def project_kernel(
    *refs, pieces, tokens, width, own, own_rows, share
):
    x_refs, refs = refs[:pieces], refs[pieces:]
    gain_ref, taps_ref, w_hbm, normed_hbm, rows_hbm, out_hbm, refs = *refs[:6], refs[6:]
    w_ref, proj_ref, block_ref, normed_ref, w_sems, out_sems, normed_sem, row_sems = refs
    me = lax.axis_index("chan")
    places = [lax.rem(me + p, pieces) for p in range(pieces)]
    total = pieces * width
    loads = [pltpu.make_async_copy(w_hbm.at[(role + 1) % 3], w_ref.at[role], w_sems.at[role]) for role in range(3)]
    for load in loads:
        load.start()
    chunk = 128
    for start in range(0, tokens, chunk):
        values = [ref[start : start + chunk, :].astype(F32) for ref in x_refs]
        mean = sum(jnp.sum(v, axis=1, keepdims=True) for v in values) / total
        centered = [v - mean for v in values]
        spread = sum(jnp.sum(c * c, axis=1, keepdims=True) for c in centered) / total
        scale = lax.rsqrt(spread + EPS)
        for p in range(pieces):
            gain = gain_ref[places[p]]
            normed_ref[p, start : start + chunk, :] = (centered[p] * scale * gain).astype(BF16)
    mine = pl.ds(pl.multiple_of(me * share, 16), share)
    keeps = [pltpu.make_async_copy(normed_ref, normed_hbm, normed_sem)]
    for p in range(pieces):
        keeps.append(pltpu.make_async_copy(x_refs[p].at[mine], rows_hbm.at[p], row_sems.at[p]))
    for keep in keeps:
        keep.start()
    step = min(width, 512)
    per_step = step // own
    parts = tokens // LANES
    proj_ref[:, :8, :] = jnp.zeros((2, 8, step), F32)
    for load in loads[:2]:
        load.wait()
    stores = []
    for col in range(0, width, step):
        cols = slice(col, col + step)
        for role in range(2):
            sums = 0.0
            for p in range(pieces):
                rows = pl.ds(pl.multiple_of(places[p] * width, width), width)
                sums = sums + matmul(normed_ref[p], w_ref[role, rows, cols])
            proj_ref[role, 8:, :] = sums.astype(BF16).astype(F32)
        shorted = []
        for role in range(2):
            value = taps_ref[0, role + 1 : role + 2, cols] * proj_ref[role, 8 : 8 + tokens, :]
            for lag in range(1, KSHORT):
                value = (
                    value
                    + taps_ref[lag, role + 1 : role + 2, cols] * proj_ref[role, 8 - lag : 8 - lag + tokens, :]
                )
            shorted.append(value)
        gated = (shorted[1] * shorted[0]).astype(BF16).T
        if col == 0:
            loads[2].wait()
            last = 0.0
            for p in range(pieces):
                rows = pl.ds(pl.multiple_of(places[p] * width, width), width)
                last = last + matmul(normed_ref[p, tokens - HALO :, :], w_ref[2, rows, :])
            last = last.astype(BF16).astype(F32)
            spread_last = [
                last[row : row + 1, lane : lane + LANES]
                for row in (HALO - 2, HALO - 1)
                for lane in range(0, width, LANES)
            ]
            spread_last = jnp.concatenate(spread_last + [jnp.zeros((8 - len(spread_last), LANES), F32)][: len(spread_last) < 8], 0)
        edges = jnp.concatenate(
            [
                proj_ref[0, 8:10, :],
                proj_ref[0, 6 + tokens : 8 + tokens, :],
                proj_ref[1, 8:10, :],
                proj_ref[1, 6 + tokens : 8 + tokens, :],
            ],
            0,
        )
        first = col // own
        for d in range(per_step):
            for part in range(parts):
                block_ref[first + d, part * own_rows : part * own_rows + own, :] = gated[
                    d * own : (d + 1) * own, part * LANES : (part + 1) * LANES
                ]
            block_edges = jnp.concatenate([edges[:, d * own : (d + 1) * own], jnp.zeros((8, LANES - own), F32)], 1)
            block_ref[first + d, parts * own_rows :, :] = jnp.concatenate([block_edges, spread_last], 0).astype(BF16)
        targets = pl.ds(first, per_step)
        store = pltpu.make_async_copy(block_ref.at[targets], out_hbm.at[targets], out_sems.at[col // step])
        store.start()
        stores.append(store)
    for store in stores:
        store.wait()
    for keep in keeps:
        keep.wait()


def gate_kernel(normed_ref, *refs, pieces, share, width, rest):
    side_refs, refs = refs[:pieces], refs[pieces:]
    w_hbm, refs = refs[:pieces], refs[pieces:]
    mix_hbm, (gate_ref, mix_ref, w_ref, rows_ref, proj_ref, w_sems, mix_sems) = refs[:pieces], refs[pieces:]
    fetches = []
    for p in range(pieces):
        size = width - rest if p == pieces - 1 else width
        fetches.append(
            pltpu.make_async_copy(
                mix_hbm[p].at[pl.ds(0, size)], mix_ref.at[pl.ds(p * width, size)], mix_sems.at[p]
            )
        )
    loads = [pltpu.make_async_copy(w_hbm[p].at[0], w_ref.at[p], w_sems.at[p]) for p in range(pieces)]
    for load in loads + fetches:
        load.start()
    me = lax.axis_index("chan")
    places = [lax.rem(me + p, pieces) for p in range(pieces)]
    mine = pl.ds(pl.multiple_of(me * share, 16), share)
    before = pl.ds(pl.multiple_of(jnp.maximum(me * share - HALO, 0), 16), HALO)
    for p in range(pieces):
        rows_ref[p, HALO:, :] = normed_ref[p, mine, :]
        rows_ref[p, :HALO, :] = normed_ref[p, before, :]
    for load in loads:
        load.wait()
    for out in range(pieces):
        sums = 0.0
        for p in range(pieces):
            rows = pl.ds(pl.multiple_of(places[p] * width, width), width)
            sums = sums + matmul(rows_ref[p], w_ref[out, rows, :])
        proj_ref[...] = sums.astype(BF16).astype(F32)
        proj_ref[HALO - 2 : HALO, :] = jnp.where(
            me == 0, side_refs[out][KSHORT : KSHORT + 2, :], proj_ref[HALO - 2 : HALO, :]
        )
        value = side_refs[out][0:1, :] * proj_ref[HALO : HALO + share, :]
        for lag in range(1, KSHORT):
            value = value + side_refs[out][lag : lag + 1, :] * proj_ref[HALO - lag : HALO - lag + share, :]
        gate_ref[out] = value.T
    for fetch in fetches:
        fetch.wait()


def filter_kernel(
    in_ref, bias_ref, mid_w_ref, out_w_ref, decay_ref, direct_ref, taps_ref,
    turn_ref, square_ref, forward_ref, spectrum_ref, own_taps_ref, own_direct_ref, gate_taps_ref,
    response_ref, columns_ref, scalars_ref, in_pad_ref, *, length, own, group
):
    padded = turn_ref.shape[1]
    seq_place = lax.axis_index("seq")
    width = out_w_ref.shape[1]
    feats = in_pad_ref.shape[0]
    in_pad_ref[...] = jnp.zeros(in_pad_ref.shape, F32)
    in_pad_ref[: in_ref.shape[0], :] = in_ref[...].astype(F32)
    in_columns = in_pad_ref[...].T.astype(BF16)
    mid_columns = mid_w_ref[...].astype(F32).T.astype(BF16)
    bias = jnp.broadcast_to(bias_ref[...], (8, bias_ref.shape[1])).T[:, :1]
    columns_ref[...] = out_w_ref[...].astype(F32).T
    scalars_ref[...] = jnp.concatenate(
        [jnp.broadcast_to(decay_ref[...], (4, width)), jnp.broadcast_to(direct_ref[...], (4, width))], 0
    ).T
    mine = pl.ds(seq_place * own, own)
    out_columns = columns_ref[mine, :].astype(BF16)
    decay = scalars_ref[mine, 0:1]
    own_direct_ref[...] = jnp.broadcast_to(scalars_ref[mine, 4:5], (own, LANES))
    shift = lax.rem(width - seq_place * own, width)
    for lag in range(KSHORT):
        own_taps = pltpu.roll(jnp.concatenate([taps_ref[lag], jnp.zeros((5, width), F32)], 0), shift, 1)
        own_taps_ref[lag] = own_taps[:, :LANES]
        gate_taps_ref[lag : lag + 1, :] = taps_ref[lag, 0:1, :]
    rows = length // LANES
    chunk = min(1024, length)
    row_ids = lax.broadcasted_iota(jnp.int32, (feats, chunk), 0)
    band = jnp.where(row_ids > BANDS, row_ids - (BANDS + 1), row_ids - 1)
    band = jnp.clip(band, 0, BANDS - 1)
    quarter = jnp.where(row_ids <= BANDS, 0.25, 0.0)
    for start in range(0, length, chunk):
        places = lax.broadcasted_iota(jnp.int32, (feats, chunk), 1) + start
        phase = lax.shift_left(places, band) & (length - 1)
        turns = phase.astype(F32) * (1.0 / length)
        waves = sine_turns(turns + quarter)
        features = jnp.where(
            row_ids == 0,
            places.astype(F32) / length,
            jnp.where(row_ids <= 2 * BANDS, waves, 0.0),
        ).astype(BF16)
        first = sine(matmul(in_columns, features) + bias).astype(BF16)
        second = sine(matmul(mid_columns, first)).astype(BF16)
        ramp = (lax.broadcasted_iota(jnp.int32, (1, chunk), 1) + start).astype(F32) / length
        response = matmul(out_columns, second) * jnp.exp(-decay * ramp)
        for part in range(chunk // LANES):
            row = start // LANES + part
            response_ref[pl.ds(row, own, stride=rows), :] = response[:, part * LANES : (part + 1) * LANES]

    def one_group(step, carry):
        def load_pair(pair):
            base = (step * group + 2 * pair) * rows
            both = [
                response_ref[pl.ds(pl.multiple_of(base + side * rows, 8), rows), :] for side in range(2)
            ]
            high, low = split_parts(jnp.concatenate(both, 1))
            return jnp.concatenate([high, low, high], 0)

        spectrum = rows_to_spectrum(
            load_pair, group, forward_ref[...], turn_ref[0], turn_ref[1], square_ref[0], square_ref[1], padded
        )
        spectrum_ref[pl.ds(pl.multiple_of(step * group * padded, 8), group * padded), :] = spectrum
        return carry

    if own == group:
        one_group(0, 0)
    else:
        lax.fori_loop(0, own // group, one_group, 0)


def convolve_kernel(
    x_ref, taps_ref, direct_ref, gate_taps_ref, spectrum_hbm, turn_hbm, square_hbm, forward_hbm, inverse_hbm, out_hbm, side_ref,
    signal_ref, result_ref, out_ref, spectrum_ref, turn_ref, square_ref, forward_ref, inverse_ref,
    load_sems, out_sems, *, length, own, own_rows, group, tokens, places
):
    padded = turn_ref.shape[1]
    sources = (forward_hbm, turn_hbm, square_hbm, inverse_hbm, spectrum_hbm)
    targets = (forward_ref, turn_ref, square_ref, inverse_ref, spectrum_ref)
    loads = [pltpu.make_async_copy(s, t, load_sems.at[k]) for k, (s, t) in enumerate(zip(sources, targets))]
    for load in loads:
        load.start()
    rows = length // LANES
    per_block = tokens // LANES
    blocks = length // tokens
    seq_place = lax.axis_index("seq")
    width = side_ref.shape[1]
    count = width // LANES
    before = x_ref[jnp.maximum(seq_place - 1, 0), per_block * own_rows :, :].astype(F32)
    before = jnp.where(seq_place > 0, before, 0.0)
    side_ref[...] = jnp.zeros(side_ref.shape, F32)
    side_ref[:KSHORT, :] = gate_taps_ref[...]
    for k in range(2 * count):
        row, lanes = KSHORT + k // count, slice(k % count * LANES, (k % count + 1) * LANES)
        side_ref[row : row + 1, lanes] = before[8 + k : 9 + k, :]
    lane = lax.broadcasted_iota(jnp.int32, (own, LANES), 1)
    fixes = []
    last = [jnp.zeros((2, LANES), F32)] * 2
    for block in range(blocks):
        edge = x_ref[block, per_block * own_rows :, :].astype(F32)
        starts = []
        for role in range(2):
            here, before = edge[4 * role : 4 * role + 2], last[role]
            two_back = jnp.concatenate([before[1:2], here[0:1]], 0)
            starts.append(
                taps_ref[0, role + 1 : role + 2, :] * here
                + taps_ref[1, role + 1 : role + 2, :] * two_back
                + taps_ref[2, role + 1 : role + 2, :] * before
            )
            last[role] = edge[4 * role + 2 : 4 * role + 4]
        fixes.append(starts[1] * starts[0])
    fixed = jnp.concatenate(fixes, 0)
    if 2 * blocks < LANES:
        fixed = jnp.concatenate([fixed, jnp.zeros((LANES - 2 * blocks, LANES), F32)], 0)
    fixed = fixed.T[:own]
    for row in range(rows):
        block, part = divmod(row, per_block)
        values = x_ref[block, part * own_rows : part * own_rows + own, :].astype(F32)
        if part == 0:
            values = jnp.where(lane == 0, fixed[:, 2 * block : 2 * block + 1], values)
            values = jnp.where(lane == 1, fixed[:, 2 * block + 1 : 2 * block + 2], values)
        signal_ref[pl.ds(row, own, stride=rows), :] = values
    for load in loads[:3]:
        load.wait()
    turn_cos, turn_sin = turn_ref[0], turn_ref[1]

    def one_group(step, carry):
        def load_pair(pair):
            base = (step * group + 2 * pair) * rows
            both = [
                signal_ref[pl.ds(pl.multiple_of(base + side * rows, 8), rows), :] for side in range(2)
            ]
            values = jnp.concatenate(both, 1).astype(BF16)
            return jnp.concatenate([values, values], 0)

        signal = rows_to_spectrum(
            load_pair, group, forward_ref[...], turn_cos, turn_sin, square_ref[0], None, padded
        )
        if own == group:
            for load in loads[3:]:
                load.wait()
        other = spectrum_ref[pl.ds(pl.multiple_of(step * group * padded, 8), group * padded), :]
        s_real, s_imag = signal[:, :LANES], signal[:, LANES:]
        f_real, f_imag = other[:, :LANES], other[:, LANES:]
        product = jnp.concatenate(
            [s_real * f_real - s_imag * f_imag, s_real * f_imag + s_imag * f_real], 1
        )
        mixed = matmul(product.astype(BF16), square_ref[2])
        for pair in range(group // 2):
            first = mixed[2 * pair * padded : (2 * pair + 1) * padded]
            second = mixed[(2 * pair + 1) * padded : (2 * pair + 2) * padded]
            real = jnp.concatenate([first[:, :LANES], second[:, :LANES]], 1)
            imag = jnp.concatenate([first[:, LANES:], second[:, LANES:]], 1)
            turned = jnp.concatenate(
                [real * turn_cos - imag * turn_sin, imag * turn_cos + real * turn_sin], 0
            )
            t_high, t_low = split_parts(turned)
            values = matmul(inverse_ref[...], jnp.concatenate([t_high, t_low, t_high], 0))
            base = (step * group + 2 * pair) * rows
            for side in range(2):
                result_ref[pl.ds(pl.multiple_of(base + side * rows, 8), rows), :] = values[
                    :, side * LANES : (side + 1) * LANES
                ]
        return carry

    if own == group:
        one_group(0, 0)
    else:
        for load in loads[3:]:
            load.wait()
        lax.fori_loop(0, own // group, one_group, 0)
    bias = direct_ref[...]
    share_rows = per_block // places
    blocks = length // tokens
    stores, half = [], max(blocks // 2, 1)
    for row in range(rows):
        block, part = divmod(row, per_block)
        place, side = divmod(part, share_rows)
        values = result_ref[pl.ds(row, own, stride=rows), :]
        values = values + bias * signal_ref[pl.ds(row, own, stride=rows), :]
        target = block * places + place
        out_ref[target, :, side * LANES : (side + 1) * LANES] = values.astype(BF16)
        if part == per_block - 1 and (block + 1) % half == 0:
            span = pl.ds((block + 1 - half) * places, half * places)
            store = pltpu.make_async_copy(out_ref.at[span], out_hbm.at[span], out_sems.at[len(stores)])
            store.start()
            stores.append(store)
    for store in stores:
        store.wait()


def gelu(values):
    return values * (lax.erf(values * np.float32(0.5**0.5)) + 1.0) * 0.5


def tail_kernel(
    z_ref, gate_ref, mix_ref, gain_ref, rows_hbm, *refs, pieces, share, width, block, rest
):
    mix_hbm, refs = refs[0], refs[1:]
    up_hbm, refs = refs[:pieces], refs[pieces:]
    down_hbm, refs = refs[:pieces], refs[pieces:]
    out_refs, refs = refs[:pieces], refs[pieces:]
    sums_ref, rows_ref, rest_ref, up_ref, down_ref, first_sems, up_sems, down_sems = refs
    total = pieces * width
    steps = up_ref.shape[2] // block
    count = pieces * steps
    firsts = [
        pltpu.make_async_copy(mix_hbm.at[pl.ds(width - rest, rest)], rest_ref, first_sems.at[0]),
        pltpu.make_async_copy(rows_hbm, rows_ref, first_sems.at[1]),
    ]
    ups, downs = [], []
    for p in range(pieces):
        for k in range(steps):
            cols = pl.ds(k * block, block)
            ups.append(pltpu.make_async_copy(up_hbm[p].at[:, cols], up_ref.at[p, :, cols], up_sems.at[p, k]))
            downs.append(pltpu.make_async_copy(down_hbm[p].at[cols], down_ref.at[p, cols], down_sems.at[p, k]))
    copies = list(firsts)
    for k in range(count + 2):
        copies += ups[k : k + 1]
        if k >= 2:
            copies.append(downs[k - 2])
    started, waited = [0], [0]

    def start_until(limit):
        while started[0] < min(limit, len(copies)):
            copies[started[0]].start()
            started[0] += 1

    def next_copy():
        start_until(waited[0] + AHEAD)
        copies[waited[0]].wait()
        waited[0] += 1

    start_until(AHEAD)
    me = lax.axis_index("chan")
    places = [lax.rem(me + p, pieces) for p in range(pieces)]
    dims = (((0,), (0,)), ((), ()))
    sums = 0.0
    for p in range(pieces):
        mixed = (z_ref[:, places[p]].reshape(width, share).astype(F32) * gate_ref[p]).astype(BF16)
        size = width - rest if p == pieces - 1 else width
        kept = mix_ref[p * width : p * width + size, :]
        sums = sums + lax.dot_general(mixed[:size], kept, dims, preferred_element_type=F32)
    next_copy()
    sums = sums + lax.dot_general(mixed[width - rest :], rest_ref[...], dims, preferred_element_type=F32)
    sums_ref[...] = sums
    next_copy()
    for p in range(pieces):
        cols = pl.ds(pl.multiple_of(places[p] * width, LANES), width)
        residual = rows_ref[p].astype(F32) + sums_ref[:, cols]
        sums_ref[:, cols] = residual.astype(BF16).astype(F32)
    values = sums_ref[...]
    mean = jnp.sum(values, axis=1, keepdims=True) / total
    centered = values - mean
    spread = jnp.sum(centered * centered, axis=1, keepdims=True) / total
    normed = (centered * lax.rsqrt(spread + EPS) * gain_ref[...]).astype(BF16)
    lifted = hidden = None
    for k in range(count + 2):
        new_lifted = new_hidden = None
        if k < count:
            next_copy()
            p, part = divmod(k, steps)
            new_lifted = matmul(normed, up_ref[p, :, part * block : (part + 1) * block])
        if lifted is not None:
            new_hidden = gelu(lifted).astype(BF16)
        if k >= 2:
            next_copy()
            p, part = divmod(k - 2, steps)
            sums_ref[...] += matmul(hidden, down_ref[p, part * block : (part + 1) * block, :])
        lifted, hidden = new_lifted, new_hidden
    for p in range(pieces):
        cols = pl.ds(pl.multiple_of(places[p] * width, LANES), width)
        out_refs[p][...] = sums_ref[:, cols].astype(BF16)


def join_kernel(*refs, pieces, share):
    out_hbm, sems = refs[pieces:]
    me = lax.axis_index("chan")
    copies = []
    for p in range(pieces):
        start = lax.rem(me + pieces - p, pieces) * share
        rows = pl.ds(pl.multiple_of(start, 16), share)
        copies.append(pltpu.make_async_copy(refs[p], out_hbm.at[rows], sems.at[p]))
    for copy in copies:
        copy.start()
    for copy in copies:
        copy.wait()


HBM = pl.BlockSpec(memory_space=pltpu.HBM)
VMEM = pl.BlockSpec(memory_space=pltpu.VMEM)


def call(kernel, in_specs, out_specs, out_shape, scratch, megabytes, *args):
    kinds = {"h": HBM, "v": VMEM, "c": VMEM}
    spaces = {"h": pltpu.HBM, "v": pltpu.VMEM, "c": pltpu.HBM}
    placed = [
        pltpu.with_memory_space_constraint(arg, spaces[kind])
        for kind, arg in zip(in_specs, args, strict=True)
    ]
    return pl.pallas_call(
        kernel,
        in_specs=[kinds[kind] for kind in in_specs],
        out_specs=out_specs,
        out_shape=out_shape,
        scratch_shapes=scratch,
        compiler_params=pltpu.CompilerParams(vmem_limit_bytes=megabytes * 1024 * 1024),
    )(*placed)


def shape_of(shape, dtype):
    return jax.ShapeDtypeStruct(shape, dtype)


def per_device(
    layer_input, gain_first, in_weight, short_weight, filt_in, filt_bias, filt_mid, filt_out,
    decay_rate, conv_bias, out_weight, gain_second, up_weight, down_weight,
):
    tokens, width = layer_input.shape
    pieces = lax.axis_size("chan")
    groups = lax.axis_size("seq")
    model = pieces * width
    length = tokens * groups
    share = tokens // pieces
    own = width // groups
    own_rows = -(-own // 16) * 16
    block_rows = tokens // LANES * own_rows + 16

    def turned(array, by):
        if by == 0:
            return array
        return lax.ppermute(array, "chan", [(i, (i - by) % pieces) for i in range(pieces)])

    def all_turned(array):
        return [turned(array, p) for p in range(pieces)]

    x_pieces = all_turned(layer_input)
    by_role = jnp.transpose(in_weight, (1, 0, 2))
    step = min(width, 512)
    normed, my_rows, gated = call(
        functools.partial(
            project_kernel, pieces=pieces, tokens=tokens, width=width, own=own, own_rows=own_rows, share=share
        ),
        "c" + "v" * (pieces - 1) + "cch",
        (HBM, HBM, HBM),
        (
            pltpu.HBM((pieces, tokens, width), BF16),
            pltpu.HBM((pieces, share, width), BF16),
            pltpu.HBM((groups, block_rows, LANES), BF16),
        ),
        [
            pltpu.VMEM((3, model, width), BF16),
            pltpu.VMEM((2, tokens + 8, step), F32),
            pltpu.VMEM((groups, block_rows, LANES), BF16),
            pltpu.VMEM((pieces, tokens, width), BF16),
            pltpu.SemaphoreType.DMA((3,)),
            pltpu.SemaphoreType.DMA((width // step,)),
            pltpu.SemaphoreType.DMA,
            pltpu.SemaphoreType.DMA((pieces,)),
        ],
        20,
        *x_pieces, gain_first.reshape(pieces, 1, width), short_weight, by_role,
    )
    by_role, out_weight, up_weight, down_weight, gated = lax.optimization_barrier(
        (by_role, out_weight, up_weight, down_weight, gated)
    )
    regrouped = lax.all_to_all(gated, "seq", split_axis=0, concat_axis=0, tiled=True)

    tables = {name: jnp.asarray(table) for name, table in transform_tables(length).items()}
    padded = tables["turn"].shape[1]
    rows = length // LANES
    filters = filt_mid.shape[0]
    spectrum, own_taps, own_direct, gate_taps = call(
        functools.partial(filter_kernel, length=length, own=own, group=own),
        "c" * 10,
        (VMEM,) * 4,
        (
            pltpu.HBM((own * padded, 2 * LANES), F32),
            pltpu.VMEM((KSHORT, 8, LANES), F32),
            pltpu.VMEM((own, LANES), F32),
            pltpu.VMEM((KSHORT, width), F32),
        ),
        [
            pltpu.VMEM((own * rows, LANES), F32),
            pltpu.VMEM((width, filters), F32),
            pltpu.VMEM((width, 8), F32),
            pltpu.VMEM((32, filters), F32),
        ],
        24,
        filt_in, filt_bias[None, :], filt_mid, filt_out, decay_rate[None, :], conv_bias[None, :],
        short_weight, tables["turn"], tables["square"], tables["forward3"],
    )
    places = pieces if share % LANES == 0 else 1
    kept_tables = [tables[name] for name in ("turn", "square", "forward2", "inverse3")]
    convolved, side = call(
        functools.partial(
            convolve_kernel, length=length, own=own, own_rows=own_rows, group=own, tokens=tokens, places=places
        ),
        "vvvv" + "h" * 5,
        (HBM, VMEM),
        (pltpu.HBM((places * groups, own, tokens // places), BF16), shape_of((8, width), F32)),
        [
            pltpu.VMEM((own * rows, LANES), F32),
            pltpu.VMEM((own * rows, LANES), F32),
            pltpu.VMEM((places * groups, own, tokens // places), BF16),
            *(pltpu.VMEM(array.shape, array.dtype) for array in (spectrum, *kept_tables)),
            pltpu.SemaphoreType.DMA((5,)),
            pltpu.SemaphoreType.DMA((2,)),
        ],
        40,
        regrouped, own_taps, own_direct, gate_taps, spectrum, *kept_tables,
    )
    if places != pieces:
        convolved = jnp.transpose(convolved.reshape(groups, own, pieces, share), (0, 2, 1, 3))
        convolved = convolved.reshape(groups * pieces, own, share)
    returned = lax.all_to_all(convolved, ("seq", "chan"), split_axis=0, concat_axis=0, tiled=True)
    returned = returned.reshape(groups, pieces, own, share)
    if own % 16:
        returned = jnp.transpose(returned, (1, 0, 2, 3)).reshape(1, pieces, width, share)

    mix_weights = all_turned(out_weight)
    up_weights = all_turned(up_weight)
    down_weights = all_turned(down_weight)
    rest = 64
    gate, mix_kept = call(
        functools.partial(gate_kernel, pieces=pieces, share=share, width=width, rest=rest),
        "c" + "v" * pieces + "h" * (2 * pieces),
        (VMEM, VMEM),
        (pltpu.VMEM((pieces, width, share), F32), pltpu.VMEM((model - rest, model), BF16)),
        [
            pltpu.VMEM((pieces, model, width), BF16),
            pltpu.VMEM((pieces, share + HALO, width), BF16),
            pltpu.VMEM((share + HALO, width), F32),
            pltpu.SemaphoreType.DMA((pieces,)),
            pltpu.SemaphoreType.DMA((pieces,)),
        ],
        16,
        normed, *all_turned(side), *all_turned(by_role), *mix_weights,
    )
    units = up_weight.shape[1]
    block = min(1024, units)
    results = call(
        functools.partial(tail_kernel, pieces=pieces, share=share, width=width, block=block, rest=rest),
        "vvvch" + "h" * (1 + 2 * pieces),
        (VMEM,) * pieces,
        tuple(shape_of((share, width), BF16) for p in range(pieces)),
        [
            pltpu.VMEM((share, model), F32),
            pltpu.VMEM((pieces, share, width), BF16),
            pltpu.VMEM((rest, model), BF16),
            pltpu.VMEM((pieces, model, units), BF16),
            pltpu.VMEM((pieces, units, model), BF16),
            pltpu.SemaphoreType.DMA((2,)),
            pltpu.SemaphoreType.DMA((pieces, units // block)),
            pltpu.SemaphoreType.DMA((pieces, units // block)),
        ],
        44,
        returned, gate, mix_kept, gain_second[None, :], my_rows, mix_weights[-1], *up_weights, *down_weights,
    )
    received = [results[0]] + [
        lax.ppermute(results[p], "chan", [(i, (i + p) % pieces) for i in range(pieces)])
        for p in range(1, pieces)
    ]
    return call(
        functools.partial(join_kernel, pieces=pieces, share=share),
        "v" * pieces,
        HBM,
        pltpu.HBM((tokens, width), BF16),
        [pltpu.SemaphoreType.DMA((pieces,))],
        8,
        *received,
    )


def solution(mesh):
    placed = (
        P("seq", "chan"),
        P(),
        P(None, None, "chan"),
        P(None, None, "chan"),
        P(),
        P(),
        P(),
        P(None, "chan"),
        P("chan"),
        P("chan"),
        P("chan", None),
        P(),
        P(None, "chan"),
        P("chan", None),
    )
    return jax.shard_map(
        per_device, mesh=mesh, in_specs=placed, out_specs=P("seq", "chan"), check_vma=False
    )
```
